32 devices in a mesh: pts: 8 (over z, x), cen: 4 (over y, core).
Axes of the slice: x: 2, y: 2, z: 4, core: 2. Of those that a mesh axis runs over, the one named last changes fastest.
Arguments:
- points: bfloat16 [16384, 768], P('pts'), may hold values from -16 to 16
- centroids: bfloat16 [4096, 768], P('cen'), may hold values from -1 to 1
Outputs:
- new_centroids: bfloat16 [4096, 768], P(('cen', 'pts'))
- distances: float32 [16384], P('pts')
The draws below stay inside these ranges and needn't reach their ends.
All inputs are finite; a program needn't handle non-finite values.
Results may differ from the reference program's by a relative error of at most 0.0034.
Values may be sent and summed in bfloat16 or wider, within the bound.
A program may use at most 64 MiB of HBM per device.

```python
import math
import jax
import jax.numpy as jnp
from jax import lax

D = 768
K = 4096
ITERS = 3
NPTS = 16384


def centroid_table(key):
    base = jax.random.fold_in(key, 7)
    table = jax.random.truncated_normal(base, -6.0, 6.0, (K, D), jnp.float32) * D ** (-0.5)
    return jnp.clip(table, -1.0, 1.0)


def draw_centroids(key, part):
    return centroid_table(key).astype(jnp.bfloat16)


def draw_points(key, part):
    base = jax.random.fold_in(key, 11)
    values = jax.random.truncated_normal(base, -6.0, 6.0, (NPTS, D), jnp.float32)
    return jnp.clip(values, -16.0, 16.0).astype(jnp.bfloat16)


def setup_inputs(seed: int = 0) -> dict:
    key_of = jax.random.split(jax.random.key(seed), 3)
    points = draw_points(jax.random.fold_in(key_of[2], 71), 0)
    centroids = draw_centroids(jax.random.fold_in(key_of[2], 71), 0)
    return dict(points=points, centroids=centroids)


sharpness = 4.0


def reference(points, centroids):
    scores = sharpness * jnp.dot(points, centroids.T, preferred_element_type=jnp.float32)
    col_potential = jnp.zeros((K,), jnp.float32)
    row_potential = jnp.zeros((NPTS,), jnp.float32)
    for iteration in range(ITERS):
        row_potential = -math.log(NPTS) - jax.nn.logsumexp(scores + col_potential[None, :], axis=1)
        col_potential = -math.log(K) - jax.nn.logsumexp(scores + row_potential[:, None], axis=0)
    blocksize = min(4096, NPTS)
    nblocks = NPTS // blocksize
    score_blocks = scores.reshape(nblocks, blocksize, K)
    potential_blocks = row_potential.reshape(nblocks, blocksize)
    point_blocks = points.reshape(nblocks, blocksize, D)

    def accumulate(carry, inputs):
        block_scores, block_rows, block_points = inputs
        transport = jnp.exp(block_scores + block_rows[:, None] + col_potential[None, :])
        weights = transport.astype(jnp.bfloat16)
        return carry + jnp.dot(weights.T, block_points, preferred_element_type=jnp.float32), None

    sums, unused = lax.scan(accumulate, jnp.zeros((K, D), jnp.float32), (score_blocks, potential_blocks, point_blocks))
    new_centroids = (K * sums).astype(jnp.bfloat16)
    squares = jnp.sum(new_centroids.astype(jnp.float32) ** 2, axis=1)

    def measure(inputs):
        block_scores, block_rows, block_points = inputs
        transport = jnp.exp(block_scores + block_rows[:, None] + col_potential[None, :])
        cross_terms = jnp.dot(block_points, new_centroids.T, preferred_element_type=jnp.float32)
        numerator = jnp.sum(transport * (squares[None, :] - 2.0 * cross_terms), axis=1)
        row_mass = jnp.sum(transport, axis=1)
        return numerator / row_mass / D

    distances = lax.map(measure, (score_blocks, potential_blocks, point_blocks)).reshape(NPTS)
    return new_centroids, distances
```

```python
import functools
import math

import jax
import jax.numpy as jnp
from jax import lax
from jax.experimental import pallas as pl
from jax.experimental.pallas import tpu as pltpu
from jax.sharding import PartitionSpec as P

ITERS = 3
SHARPNESS = 4.0
LOG2E = 1.4426950408889634
LANES = 128
NT = (((1,), (1,)), ((), ()))
NN = (((1,), (0,)), ((), ()))


def log2(value):
    return jnp.log(value) * LOG2E


def merged_lse(parts):
    highest = jnp.max(parts, axis=0)
    return highest + log2(jnp.sum(jnp.exp2(parts - highest[None]), axis=0))


def remote(src, dst, send, recv, axis, index):
    return pltpu.make_async_remote_copy(
        src_ref=src, dst_ref=dst, send_sem=send, recv_sem=recv,
        device_id={axis: index}, device_id_type=pl.DeviceIdType.MESH,
    )


def exchange(slots, send, recv, axis, count):
    me = lax.axis_index(axis)

    def copy_to(step):
        peer = lax.rem(me + step, count)
        return remote(slots.at[me], slots.at[me], send.at[peer], recv.at[me], axis, peer)

    def copy_from(step):
        peer = lax.rem(me + step, count)
        return remote(slots.at[peer], slots.at[peer], send.at[peer], recv.at[peer], axis, peer)

    @pl.loop(1, count)
    def _(step):
        copy_to(step).start()

    @pl.loop(1, count)
    def _(step):
        copy_from(step).wait_recv()

    @pl.loop(1, count)
    def _(step):
        copy_to(step).wait_send()


def kernel(
    n_pts, n_cen, total_points, total_centroids,
    points, centroids, new_block, distances,
    scores, weights, products, row_slots, col_slots, final_slots, row_rep, col_rep, part_max, part_sum,
    mass_acc, num_acc, x_out, x_in, z_out, z_in, gathered,
    row_send, row_recv, col_send, col_recv, final_send, final_recv,
    xs_sem, xr_sem, zs_sem, zr_sem, gxs_sem, gxr_sem, gzs_sem, gzr_sem,
):
    n_i, width = points.shape
    n_k = centroids.shape[0]
    rows = n_k // n_pts
    pair = 2 * rows
    groups = n_pts // 2
    i_chunks = n_i // LANES
    k_chunks = n_k // LANES
    me = lax.axis_index("pts")
    mine = lax.axis_index("cen")
    hi = me // 2
    lo = lax.rem(me, 2)
    other = 1 - lo

    barrier = pltpu.get_barrier_semaphore()

    @pl.loop(1, n_pts)
    def _(step):
        pl.semaphore_signal(
            barrier, inc=1, device_id={"pts": lax.rem(me + step, n_pts)}, device_id_type=pl.DeviceIdType.MESH
        )

    @pl.loop(1, n_cen)
    def _(step):
        pl.semaphore_signal(
            barrier, inc=1, device_id={"cen": lax.rem(mine + step, n_cen)}, device_id_type=pl.DeviceIdType.MESH
        )

    def row_lse(start, slot, shifted):
        highest = [None, None]
        total = [None, None]
        for k in range(k_chunks):
            for half in range(2):
                block = scores[pl.ds(k * LANES, LANES), pl.ds(start + half * LANES, LANES)]
                if shifted:
                    block = block + col_rep[pl.ds(k * LANES, LANES), :]
                block = block.reshape(LANES // 8, 8, LANES)
                top = jnp.max(block, axis=0)
                if highest[half] is None:
                    total[half] = jnp.sum(jnp.exp2(block - top[None]), axis=0)
                else:
                    top = jnp.maximum(highest[half], top)
                    total[half] = total[half] * jnp.exp2(highest[half] - top) + jnp.sum(
                        jnp.exp2(block - top[None]), axis=0
                    )
                highest[half] = top
        for half in range(2):
            top = jnp.max(highest[half], axis=0, keepdims=True)
            summed = jnp.sum(total[half] * jnp.exp2(highest[half] - top), axis=0, keepdims=True)
            slot[pl.ds(start // LANES + half, 1), :] = top + log2(summed)

    for iteration in range(ITERS):
        slots = row_slots.at[iteration]

        @pl.loop(0, i_chunks // 2)
        def _(chunk):
            start = pl.multiple_of(chunk * 2 * LANES, 2 * LANES)
            if iteration == 0:
                product = lax.dot_general(
                    centroids[...], points[pl.ds(start, 2 * LANES), :], NT, preferred_element_type=jnp.float32
                )
                scores[:, pl.ds(start, 2 * LANES)] = product * (SHARPNESS * LOG2E)
            row_lse(start, slots.at[mine], iteration > 0)

        if iteration == 0:
            pl.semaphore_wait(barrier, n_pts + n_cen - 2)
        exchange(slots, row_send.at[iteration], row_recv.at[iteration], "cen", n_cen)
        row_potential = -math.log2(total_points) - merged_lse(slots[...])
        for chunk in range(i_chunks):
            row_rep[:, pl.ds(chunk * LANES, LANES)] = jnp.broadcast_to(
                row_potential[chunk : chunk + 1, :], (8, LANES)
            )

        @pl.loop(0, n_k // 16)
        def _(group):
            start = pl.multiple_of(group * 16, 16)
            parts = [
                scores[pl.ds(start, 16), pl.ds(chunk * LANES, LANES)].reshape(2, 8, LANES)
                + row_rep[:, pl.ds(chunk * LANES, LANES)][None]
                for chunk in range(i_chunks)
            ]
            top = functools.reduce(jnp.maximum, parts)
            total = functools.reduce(jnp.add, [jnp.exp2(part - top) for part in parts])
            part_max[pl.ds(start, 16), :] = top.reshape(16, LANES)
            part_sum[pl.ds(start, 16), :] = total.reshape(16, LANES)

        slots = col_slots.at[iteration]
        for chunk in range(k_chunks):
            tops = part_max[pl.ds(chunk * LANES, LANES), :].T
            sums = part_sum[pl.ds(chunk * LANES, LANES), :].T
            top = jnp.max(tops, axis=0, keepdims=True)
            summed = jnp.sum(sums * jnp.exp2(tops - top), axis=0, keepdims=True)
            slots[me, pl.ds(chunk, 1), :] = top + log2(summed)
        exchange(slots, col_send.at[iteration], col_recv.at[iteration], "pts", n_pts)
        col_potential = -math.log2(total_centroids) - merged_lse(slots[...])
        for chunk in range(k_chunks):
            col_rep[pl.ds(chunk * LANES, LANES), :] = jnp.broadcast_to(
                col_potential[chunk : chunk + 1, :], (LANES, LANES)
            ).T

    mass_acc[...] = jnp.zeros_like(mass_acc)
    num_acc[...] = jnp.zeros_like(num_acc)

    def x_copy(group):
        return remote(x_out.at[group], x_in.at[group], xs_sem.at[group], xr_sem.at[group], "pts", 2 * hi + other)

    def z_copy_to(group):
        return remote(z_out.at[group], z_in.at[hi], zs_sem.at[group], zr_sem.at[hi], "pts", 2 * group + lo)

    def z_copy_from(group):
        return remote(z_out.at[group], z_in.at[group], zs_sem.at[group], zr_sem.at[group], "pts", 2 * group + lo)

    @pl.loop(0, groups)
    def _(step):
        group = lax.rem(hi + step + 1, groups)
        base = pl.multiple_of(group * pair, pair)

        @pl.loop(0, pair // 16)
        def _(sub):
            start = pl.multiple_of(base + sub * 16, 16)
            for chunk in range(i_chunks):
                lanes = pl.ds(chunk * LANES, LANES)
                value = (
                    scores[pl.ds(start, 16), lanes].reshape(2, 8, LANES)
                    + row_rep[:, lanes][None]
                    + col_rep[pl.ds(start, 16), :].reshape(2, 8, LANES)
                )
                value = jnp.exp2(value)
                mass_acc[:, lanes] += value[0] + value[1]
                value = value.reshape(16, LANES)
                scores[pl.ds(start, 16), lanes] = value
                weights[pl.ds(start, 16), lanes] = value.astype(jnp.bfloat16)

        products[group] = lax.dot_general(
            weights[pl.ds(base, pair), :], points[...], NN, preferred_element_type=jnp.float32
        )
        x_out[group] = products[group, pl.ds(pl.multiple_of(other * rows, rows), rows), :].astype(jnp.bfloat16)
        x_copy(group).start()

    own_half = pl.ds(pl.multiple_of(lo * rows, rows), rows)

    @pl.loop(0, groups - 1)
    def _(step):
        group = lax.rem(hi + step + 1, groups)
        x_copy(group).wait_recv()
        z_out[group] = (products[group, own_half, :] + x_in[group].astype(jnp.float32)).astype(jnp.bfloat16)
        z_copy_to(group).start()

    x_copy(hi).wait_recv()
    products[hi, own_half, :] = products[hi, own_half, :] + x_in[hi].astype(jnp.float32)

    @pl.loop(0, groups - 1)
    def _(step):
        group = lax.rem(hi + step + 1, groups)
        z_copy_from(group).wait_recv()
        products[hi, own_half, :] = products[hi, own_half, :] + z_in[group].astype(jnp.float32)

    finished = (products[hi, own_half, :] * float(total_centroids)).astype(jnp.bfloat16)
    new_block[...] = finished
    gathered[me] = finished

    def gx_copy(group, side):
        block = gathered.at[2 * group + side]
        return remote(block, block, gxs_sem.at[group], gxr_sem.at[group], "pts", 2 * hi + other)

    def gz_copy_to(group):
        block = gathered.at[me]
        return remote(block, block, gzs_sem.at[group], gzr_sem.at[hi], "pts", 2 * group + lo)

    def gz_copy_from(group):
        block = gathered.at[2 * group + lo]
        return remote(block, block, gzs_sem.at[group], gzr_sem.at[group], "pts", 2 * group + lo)

    gx_copy(hi, lo).start()

    @pl.loop(0, groups - 1)
    def _(step):
        gz_copy_to(lax.rem(hi + step + 1, groups)).start()

    def pair_terms(group):
        base = pl.multiple_of(group * pair, pair)
        block = gathered[pl.ds(2 * group, 2)].reshape(pair, width)
        wide = block.astype(jnp.float32)
        squares = jnp.sum(wide * wide, axis=1, keepdims=True)

        @pl.loop(0, n_i // 512)
        def _(chunk):
            lanes = pl.ds(pl.multiple_of(chunk * 512, 512), 512)
            cross = lax.dot_general(block, points[lanes, :], NT, preferred_element_type=jnp.float32)
            terms = scores[pl.ds(base, pair), lanes] * (squares - 2.0 * cross)
            num_acc[:, lanes] += jnp.sum(terms.reshape(pair // 8, 8, 512), axis=0)

    @pl.loop(0, groups)
    def _(step):
        following = lax.rem(hi + groups - step - 1, groups)
        group = lax.rem(hi + groups - step, groups)

        @pl.when(step < groups - 1)
        def _():
            gz_copy_from(following).wait_recv()
            gx_copy(following, lo).start()

        gx_copy(group, other).wait_recv()
        pair_terms(group)

    final = final_slots.at[mine]
    for chunk in range(i_chunks):
        lanes = pl.ds(chunk * LANES, LANES)
        final[pl.ds(chunk, 1), :] = jnp.sum(num_acc[:, lanes], axis=0, keepdims=True)
        final[pl.ds(i_chunks + chunk, 1), :] = jnp.sum(mass_acc[:, lanes], axis=0, keepdims=True)
    exchange(final_slots, final_send, final_recv, "cen", n_cen)
    sums = jnp.sum(final_slots[...], axis=0)
    distances[...] = sums[:i_chunks] / sums[i_chunks:] / float(width)

    @pl.loop(0, groups)
    def _(step):
        x_copy(step).wait_send()
        gx_copy(step, lo).wait_send()

    @pl.loop(0, groups - 1)
    def _(step):
        group = lax.rem(hi + step + 1, groups)
        z_copy_to(group).wait_send()
        gz_copy_to(group).wait_send()


def on_device(n_pts, n_cen, points, centroids):
    n_i, width = points.shape
    n_k = centroids.shape[0]
    rows, groups = n_k // n_pts, n_pts // 2
    i_chunks, k_chunks = n_i // LANES, n_k // LANES
    f32, bf16 = jnp.float32, jnp.bfloat16
    vmem, dma = pltpu.VMEM, pltpu.SemaphoreType.DMA
    whole = pl.BlockSpec(memory_space=pltpu.VMEM)
    new_block, distances = pl.pallas_call(
        functools.partial(kernel, n_pts, n_cen, n_i * n_pts, n_k * n_cen),
        out_shape=(
            jax.ShapeDtypeStruct((rows, width), bf16),
            jax.ShapeDtypeStruct((i_chunks, LANES), f32),
        ),
        in_specs=[whole, whole],
        out_specs=(whole, whole),
        scratch_shapes=[
            vmem((n_k, n_i), f32),
            vmem((n_k, n_i), bf16),
            vmem((groups, 2 * rows, width), f32),
            vmem((ITERS, n_cen, i_chunks, LANES), f32),
            vmem((ITERS, n_pts, k_chunks, LANES), f32),
            vmem((n_cen, 2 * i_chunks, LANES), f32),
            vmem((8, n_i), f32),
            vmem((n_k, LANES), f32),
            vmem((n_k, LANES), f32),
            vmem((n_k, LANES), f32),
            vmem((8, n_i), f32),
            vmem((8, n_i), f32),
            vmem((groups, rows, width), bf16),
            vmem((groups, rows, width), bf16),
            vmem((groups, rows, width), bf16),
            vmem((groups, rows, width), bf16),
            vmem((n_pts, rows, width), bf16),
            dma((ITERS, n_cen)), dma((ITERS, n_cen)),
            dma((ITERS, n_pts)), dma((ITERS, n_pts)),
            dma((n_cen,)), dma((n_cen,)),
            *[dma((groups,)) for _ in range(8)],
        ],
        compiler_params=pltpu.CompilerParams(
            collective_id=0, has_side_effects=True, vmem_limit_bytes=52 * 2**20
        ),
        cost_estimate=pl.CostEstimate(
            flops=6 * n_i * n_k * width, bytes_accessed=2 * (n_i + n_k) * width, transcendentals=7 * n_i * n_k
        ),
    )(points, centroids)
    return new_block, distances.reshape(n_i)


def solution(mesh):
    n_pts, n_cen = mesh.shape["pts"], mesh.shape["cen"]
    return jax.shard_map(
        functools.partial(on_device, n_pts, n_cen),
        mesh=mesh,
        in_specs=(P("pts", None), P("cen", None)),
        out_specs=(P(("cen", "pts"), None), P("pts")),
        check_vma=False,
    )
```

```python
import functools
import math

import jax
import jax.numpy as jnp
from jax import lax
from jax.experimental import pallas as pl
from jax.experimental.pallas import tpu as pltpu
from jax.sharding import PartitionSpec as P

ITERS = 3
SHARPNESS = 4.0
LOG2E = 1.4426950408889634
LANES = 128
NT = (((1,), (1,)), ((), ()))
NN = (((1,), (0,)), ((), ()))


def log2(value):
    return jnp.log(value) * LOG2E


def merged_lse(parts):
    highest = jnp.max(parts, axis=0)
    return highest + log2(jnp.sum(jnp.exp2(parts - highest[None]), axis=0))


def remote(src, dst, send, recv, axis, index):
    return pltpu.make_async_remote_copy(
        src_ref=src, dst_ref=dst, send_sem=send, recv_sem=recv,
        device_id={axis: index}, device_id_type=pl.DeviceIdType.MESH,
    )


def each(start, stop, body):
    if stop - start <= 8:
        for step in range(start, stop):
            body(step)
    else:
        pl.loop(start, stop)(body)


def tree(join, values):
    values = list(values)
    while len(values) > 1:
        paired = [join(a, b) for a, b in zip(values[::2], values[1::2])]
        values = paired + values[len(values) & ~1 :]
    return values[0]


def exchange(slots, send, recv, axis, count):
    me = lax.axis_index(axis)

    def copy_to(step):
        peer = lax.rem(me + step, count)
        return remote(slots.at[me], slots.at[me], send.at[peer], recv.at[me], axis, peer)

    def copy_from(step):
        peer = lax.rem(me + step, count)
        return remote(slots.at[peer], slots.at[peer], send.at[peer], recv.at[peer], axis, peer)

    each(1, count, lambda step: copy_to(step).start())
    each(1, count, lambda step: copy_from(step).wait_recv())
    each(1, count, lambda step: copy_to(step).wait_send())


def kernel(
    n_pts, n_cen, total_points, total_centroids,
    points, centroids, new_block, distances,
    scores, weights, products, row_slots, col_slots, final_slots, row_rep, col_rep, part_max, part_sum,
    mass_acc, num_acc, x_out, x_in, z_out, z_in, gathered,
    row_send, row_recv, col_send, col_recv, final_send, final_recv,
    xs_sem, xr_sem, zs_sem, zr_sem, gxs_sem, gxr_sem, gzs_sem, gzr_sem,
):
    n_i, width = points.shape
    n_k = centroids.shape[0]
    rows = n_k // n_pts
    pair = 2 * rows
    parts, piece = gathered.shape[0], gathered.shape[3]
    groups = n_pts // 2
    i_chunks = n_i // LANES
    k_chunks = n_k // LANES
    me = lax.axis_index("pts")
    mine = lax.axis_index("cen")
    hi = me // 2
    lo = lax.rem(me, 2)
    other = 1 - lo

    barrier = pltpu.get_barrier_semaphore()

    @pl.loop(1, n_pts)
    def _(step):
        pl.semaphore_signal(
            barrier, inc=1, device_id={"pts": lax.rem(me + step, n_pts)}, device_id_type=pl.DeviceIdType.MESH
        )

    @pl.loop(1, n_cen)
    def _(step):
        pl.semaphore_signal(
            barrier, inc=1, device_id={"cen": lax.rem(mine + step, n_cen)}, device_id_type=pl.DeviceIdType.MESH
        )

    def row_lse(start, slot, block_of):
        highest = [None, None]
        total = [None, None]
        for k in range(k_chunks):
            for half in range(2):
                block = block_of(k, half)
                parts = [block[8 * n : 8 * n + 8] for n in range(LANES // 8)]
                top = tree(jnp.maximum, parts)
                if highest[half] is not None:
                    top = jnp.maximum(highest[half], top)
                summed = tree(jnp.add, [jnp.exp2(part - top) for part in parts])
                if highest[half] is not None:
                    summed = total[half] * jnp.exp2(highest[half] - top) + summed
                highest[half], total[half] = top, summed
        for half in range(2):
            top = jnp.max(highest[half], axis=0, keepdims=True)
            summed = jnp.sum(total[half] * jnp.exp2(highest[half] - top), axis=0, keepdims=True)
            slot[pl.ds(start // LANES + half, 1), :] = top + log2(summed)

    def first_blocks(start):
        columns = points[pl.ds(start, 2 * LANES), :]
        products_of = {}

        def block_of(k, half):
            if k % 2 == 0 and half == 0:
                product = lax.dot_general(
                    centroids[pl.ds(k * LANES, 2 * LANES), :], columns, NT, preferred_element_type=jnp.float32
                ) * (SHARPNESS * LOG2E)
                scores[pl.ds(k * LANES, 2 * LANES), pl.ds(start, 2 * LANES)] = product
                products_of[k // 2] = product
            lines = slice((k % 2) * LANES, (k % 2 + 1) * LANES)
            return products_of[k // 2][lines, half * LANES : (half + 1) * LANES]

        return block_of

    def shifted_blocks(start):
        def block_of(k, half):
            lines = pl.ds(k * LANES, LANES)
            return scores[lines, pl.ds(start + half * LANES, LANES)] + col_rep[lines, :]

        return block_of

    for iteration in range(ITERS):
        slots = row_slots.at[iteration]

        @pl.loop(0, i_chunks // 2)
        def _(chunk):
            start = pl.multiple_of(chunk * 2 * LANES, 2 * LANES)
            row_lse(start, slots.at[mine], shifted_blocks(start) if iteration else first_blocks(start))

        if iteration == 0:
            pl.semaphore_wait(barrier, n_pts + n_cen - 2)
        exchange(slots, row_send.at[iteration], row_recv.at[iteration], "cen", n_cen)
        row_potential = -math.log2(total_points) - merged_lse(slots[...])
        for chunk in range(i_chunks):
            row_rep[:, pl.ds(chunk * LANES, LANES)] = jnp.broadcast_to(
                row_potential[chunk : chunk + 1, :], (8, LANES)
            )

        @pl.loop(0, n_k // 16, unroll=2)
        def _(group):
            start = pl.multiple_of(group * 16, 16)
            parts = [
                scores[pl.ds(start, 16), pl.ds(chunk * LANES, LANES)].reshape(2, 8, LANES)
                + row_rep[:, pl.ds(chunk * LANES, LANES)][None]
                for chunk in range(i_chunks)
            ]
            top = tree(jnp.maximum, parts)
            total = tree(jnp.add, [jnp.exp2(part - top) for part in parts])
            part_max[pl.ds(start, 16), :] = top.reshape(16, LANES)
            part_sum[pl.ds(start, 16), :] = total.reshape(16, LANES)

        slots = col_slots.at[iteration]
        for chunk in range(k_chunks):
            tops = part_max[pl.ds(chunk * LANES, LANES), :].T
            sums = part_sum[pl.ds(chunk * LANES, LANES), :].T
            top = jnp.max(tops, axis=0, keepdims=True)
            summed = jnp.sum(sums * jnp.exp2(tops - top), axis=0, keepdims=True)
            slots[me, pl.ds(chunk, 1), :] = top + log2(summed)
        exchange(slots, col_send.at[iteration], col_recv.at[iteration], "pts", n_pts)
        col_potential = -math.log2(total_centroids) - merged_lse(slots[...])
        for chunk in range(k_chunks):
            col_rep[pl.ds(chunk * LANES, LANES), :] = jnp.broadcast_to(
                col_potential[chunk : chunk + 1, :], (LANES, LANES)
            ).T

    mass_acc[...] = jnp.zeros_like(mass_acc)
    num_acc[...] = jnp.zeros_like(num_acc)

    def x_copy(part, group):
        return remote(
            x_out.at[part, group], x_in.at[part, group], xs_sem.at[part, group], xr_sem.at[part, group],
            "pts", 2 * hi + other,
        )

    def z_copy_to(part, group):
        return remote(
            z_out.at[part, group], z_in.at[part, hi], zs_sem.at[part, group], zr_sem.at[part, hi],
            "pts", 2 * group + lo,
        )

    def z_copy_from(part, group):
        return remote(
            z_out.at[part, group], z_in.at[part, group], zs_sem.at[part, group], zr_sem.at[part, group],
            "pts", 2 * group + lo,
        )

    def gx_copy(part, group, side):
        block = gathered.at[part, 2 * group + side]
        return remote(block, block, gxs_sem.at[part, group], gxr_sem.at[part, group], "pts", 2 * hi + other)

    def gz_copy_to(part, group):
        block = gathered.at[part, me]
        return remote(block, block, gzs_sem.at[part, group], gzr_sem.at[part, hi], "pts", 2 * group + lo)

    def gz_copy_from(part, group):
        block = gathered.at[part, 2 * group + lo]
        return remote(block, block, gzs_sem.at[part, group], gzr_sem.at[part, group], "pts", 2 * group + lo)

    def later(step):
        return lax.rem(hi + step + 1, groups)

    def earlier(step):
        return lax.rem(hi + groups - step - 1, groups)

    own_half = pl.ds(pl.multiple_of(lo * rows, rows), rows)
    other_half = pl.ds(pl.multiple_of(other * rows, rows), rows)

    def columns_of(part):
        return slice(part * piece, (part + 1) * piece)

    def plan(group):
        base = pl.multiple_of(group * pair, pair)

        @pl.loop(0, pair // 16)
        def _(sub):
            start = pl.multiple_of(base + sub * 16, 16)
            for chunk in range(i_chunks):
                lanes = pl.ds(chunk * LANES, LANES)
                value = (
                    scores[pl.ds(start, 16), lanes].reshape(2, 8, LANES)
                    + row_rep[:, lanes][None]
                    + col_rep[pl.ds(start, 16), :].reshape(2, 8, LANES)
                )
                value = jnp.exp2(value)
                mass_acc[:, lanes] += value[0] + value[1]
                value = value.reshape(16, LANES)
                scores[pl.ds(start, 16), lanes] = value
                weights[pl.ds(start, 16), lanes] = value.astype(jnp.bfloat16)

    def produce(part):
        @pl.loop(0, groups)
        def _(step):
            group = later(step)
            if part == 0:
                plan(group)
            base = pl.multiple_of(group * pair, pair)
            products[part, group] = lax.dot_general(
                weights[pl.ds(base, pair), :], points[:, columns_of(part)], NN, preferred_element_type=jnp.float32
            )
            x_out[part, group] = products[part, group, other_half, :].astype(jnp.bfloat16)
            x_copy(part, group).start()

    def reduce_pair(part):
        @pl.loop(0, groups - 1)
        def _(step):
            group = later(step)
            x_copy(part, group).wait_recv()
            z_out[part, group] = (
                products[part, group, own_half, :] + x_in[part, group].astype(jnp.float32)
            ).astype(jnp.bfloat16)
            z_copy_to(part, group).start()

    def finish(part):
        x_copy(part, hi).wait_recv()
        products[part, hi, own_half, :] = products[part, hi, own_half, :] + x_in[part, hi].astype(jnp.float32)

        @pl.loop(0, groups - 1)
        def _(step):
            group = earlier(step)
            z_copy_from(part, group).wait_recv()
            products[part, hi, own_half, :] = products[part, hi, own_half, :] + z_in[part, group].astype(jnp.float32)

        done = (products[part, hi, own_half, :] * float(total_centroids)).astype(jnp.bfloat16)
        new_block[:, columns_of(part)] = done
        gathered[part, me] = done
        gx_copy(part, hi, lo).start()

        @pl.loop(0, groups - 1)
        def _(step):
            gz_copy_to(part, later(step)).start()

    def hand_on(part):
        @pl.loop(0, groups - 1)
        def _(step):
            group = earlier(step)
            gz_copy_from(part, group).wait_recv()
            gx_copy(part, group, lo).start()

    def cross(part):
        @pl.loop(0, groups)
        def _(step):
            group = lax.rem(hi + groups - step, groups)
            gx_copy(part, group, other).wait_recv()
            base = pl.multiple_of(group * pair, pair)
            block = gathered[part, pl.ds(2 * group, 2)].reshape(pair, piece)
            wide = block.astype(jnp.float32)
            squares = jnp.sum(wide * wide, axis=1, keepdims=True)
            doubled = (wide * -2.0).astype(jnp.bfloat16)

            @pl.loop(0, n_i // 512)
            def _(chunk):
                lanes = pl.ds(pl.multiple_of(chunk * 512, 512), 512)
                product = lax.dot_general(
                    doubled, points[lanes, columns_of(part)], NT, preferred_element_type=jnp.float32
                )
                terms = scores[pl.ds(base, pair), lanes] * (squares + product)
                num_acc[:, lanes] += jnp.sum(terms.reshape(pair // 8, 8, 512), axis=0)

    produce(0)
    for part in range(1, parts):
        produce(part)
        reduce_pair(part - 1)
        if part >= 2:
            finish(part - 2)
    reduce_pair(parts - 1)
    if parts >= 2:
        finish(parts - 2)
        hand_on(0)
    finish(parts - 1)
    for part in range(parts):
        if part or parts == 1:
            hand_on(part)
        cross(part)

    final = final_slots.at[mine]
    for chunk in range(i_chunks):
        lanes = pl.ds(chunk * LANES, LANES)
        final[pl.ds(chunk, 1), :] = jnp.sum(num_acc[:, lanes], axis=0, keepdims=True)
        final[pl.ds(i_chunks + chunk, 1), :] = jnp.sum(mass_acc[:, lanes], axis=0, keepdims=True)
    exchange(final_slots, final_send, final_recv, "cen", n_cen)
    sums = jnp.sum(final_slots[...], axis=0)
    distances[...] = sums[:i_chunks] / sums[i_chunks:] / float(width)

    for part in range(parts):

        @pl.loop(0, groups)
        def _(step):
            x_copy(part, step).wait_send()
            gx_copy(part, step, lo).wait_send()

        @pl.loop(0, groups - 1)
        def _(step):
            z_copy_to(part, later(step)).wait_send()
            gz_copy_to(part, later(step)).wait_send()


def on_device(n_pts, n_cen, points, centroids):
    n_i, width = points.shape
    n_k = centroids.shape[0]
    rows, groups = n_k // n_pts, n_pts // 2
    i_chunks, k_chunks = n_i // LANES, n_k // LANES
    parts = 3 if width % (3 * LANES) == 0 else 1
    piece = width // parts
    f32, bf16 = jnp.float32, jnp.bfloat16
    vmem, dma = pltpu.VMEM, pltpu.SemaphoreType.DMA
    whole = pl.BlockSpec(memory_space=pltpu.VMEM)
    new_block, distances = pl.pallas_call(
        functools.partial(kernel, n_pts, n_cen, n_i * n_pts, n_k * n_cen),
        out_shape=(
            jax.ShapeDtypeStruct((rows, width), bf16),
            jax.ShapeDtypeStruct((i_chunks, LANES), f32),
        ),
        in_specs=[whole, whole],
        out_specs=(whole, whole),
        scratch_shapes=[
            vmem((n_k, n_i), f32),
            vmem((n_k, n_i), bf16),
            vmem((parts, groups, 2 * rows, piece), f32),
            vmem((ITERS, n_cen, i_chunks, LANES), f32),
            vmem((ITERS, n_pts, k_chunks, LANES), f32),
            vmem((n_cen, 2 * i_chunks, LANES), f32),
            vmem((8, n_i), f32),
            vmem((n_k, LANES), f32),
            vmem((n_k, LANES), f32),
            vmem((n_k, LANES), f32),
            vmem((8, n_i), f32),
            vmem((8, n_i), f32),
            vmem((parts, groups, rows, piece), bf16),
            vmem((parts, groups, rows, piece), bf16),
            vmem((parts, groups, rows, piece), bf16),
            vmem((parts, groups, rows, piece), bf16),
            vmem((parts, n_pts, rows, piece), bf16),
            dma((ITERS, n_cen)), dma((ITERS, n_cen)),
            dma((ITERS, n_pts)), dma((ITERS, n_pts)),
            dma((n_cen,)), dma((n_cen,)),
            *[dma((parts, groups)) for _ in range(8)],
        ],
        compiler_params=pltpu.CompilerParams(
            collective_id=0, has_side_effects=True, vmem_limit_bytes=52 * 2**20
        ),
        cost_estimate=pl.CostEstimate(
            flops=6 * n_i * n_k * width, bytes_accessed=2 * (n_i + n_k) * width, transcendentals=7 * n_i * n_k
        ),
    )(points, centroids)
    return new_block, distances.reshape(n_i)


def solution(mesh):
    n_pts, n_cen = mesh.shape["pts"], mesh.shape["cen"]
    return jax.shard_map(
        functools.partial(on_device, n_pts, n_cen),
        mesh=mesh,
        in_specs=(P("pts", None), P("cen", None)),
        out_specs=(P(("cen", "pts"), None), P("pts")),
        check_vma=False,
    )
```

```python
import functools
import math

import jax
import jax.numpy as jnp
from jax import lax
from jax.experimental import pallas as pl
from jax.experimental.pallas import tpu as pltpu
from jax.sharding import PartitionSpec as P

ITERS = 3
SHARPNESS = 4.0
LOG2E = 1.4426950408889634
LANES = 128
NT = (((1,), (1,)), ((), ()))
NN = (((1,), (0,)), ((), ()))


def log2(value):
    return jnp.log(value) * LOG2E


def merged_lse(parts):
    highest = jnp.max(parts, axis=0)
    return highest + log2(jnp.sum(jnp.exp2(parts - highest[None]), axis=0))


def remote(src, dst, send, recv, axis, index):
    return pltpu.make_async_remote_copy(
        src_ref=src, dst_ref=dst, send_sem=send, recv_sem=recv,
        device_id={axis: index}, device_id_type=pl.DeviceIdType.MESH,
    )


def each(start, stop, body):
    if stop - start <= 8:
        for step in range(start, stop):
            body(step)
    else:
        pl.loop(start, stop)(body)


def tree(join, values):
    values = list(values)
    while len(values) > 1:
        paired = [join(a, b) for a, b in zip(values[::2], values[1::2])]
        values = paired + values[len(values) & ~1 :]
    return values[0]


def exchange(slots, send, recv, axis, count):
    me = lax.axis_index(axis)

    def copy_to(step):
        peer = lax.rem(me + step, count)
        return remote(slots.at[me], slots.at[me], send.at[peer], recv.at[me], axis, peer)

    def copy_from(step):
        peer = lax.rem(me + step, count)
        return remote(slots.at[peer], slots.at[peer], send.at[peer], recv.at[peer], axis, peer)

    each(1, count, lambda step: copy_to(step).start())
    each(1, count, lambda step: copy_from(step).wait_recv())
    each(1, count, lambda step: copy_to(step).wait_send())


def kernel(
    scaled, n_pts, n_cen, total_points, total_centroids,
    points, centroids, new_block, distances,
    scores, weights, products, row_slots, col_slots, final_slots, row_rep, col_rep, part_max, part_sum, row_share,
    mass_acc, num_acc, x_out, x_in, z_out, z_in, gathered,
    row_send, row_recv, col_send, col_recv, final_send, final_recv,
    xs_sem, xr_sem, zs_sem, zr_sem, gxs_sem, gxr_sem, gzs_sem, gzr_sem,
):
    n_i, width = points.shape
    n_k = centroids.shape[0]
    rows = n_k // n_pts
    pair = 2 * rows
    parts, piece = gathered.shape[0], gathered.shape[3]
    groups = n_pts // 2
    i_chunks = n_i // LANES
    k_chunks = n_k // LANES
    me = lax.axis_index("pts")
    mine = lax.axis_index("cen")
    hi = me // 2
    lo = lax.rem(me, 2)
    other = 1 - lo

    barrier = pltpu.get_barrier_semaphore()

    @pl.loop(1, n_pts)
    def _(step):
        pl.semaphore_signal(
            barrier, inc=1, device_id={"pts": lax.rem(me + step, n_pts)}, device_id_type=pl.DeviceIdType.MESH
        )

    @pl.loop(1, n_cen)
    def _(step):
        pl.semaphore_signal(
            barrier, inc=1, device_id={"cen": lax.rem(mine + step, n_cen)}, device_id_type=pl.DeviceIdType.MESH
        )

    def row_lse(start, slot, block_of):
        highest = [None, None]
        total = [None, None]
        for k in range(k_chunks):
            for half in range(2):
                block = block_of(k, half)
                parts = [block[8 * n : 8 * n + 8] for n in range(LANES // 8)]
                top = tree(jnp.maximum, parts)
                if highest[half] is not None:
                    top = jnp.maximum(highest[half], top)
                summed = tree(jnp.add, [jnp.exp2(part - top) for part in parts])
                if highest[half] is not None:
                    summed = total[half] * jnp.exp2(highest[half] - top) + summed
                highest[half], total[half] = top, summed
        for half in range(2):
            top = jnp.max(highest[half], axis=0, keepdims=True)
            summed = jnp.sum(total[half] * jnp.exp2(highest[half] - top), axis=0, keepdims=True)
            slot[pl.ds(start // LANES + half, 1), :] = top + log2(summed)

    def first_blocks(start):
        columns = points[pl.ds(start, 2 * LANES), :]
        products_of = {}

        def block_of(k, half):
            if k % 2 == 0 and half == 0:
                product = lax.dot_general(
                    centroids[pl.ds(k * LANES, 2 * LANES), :], columns, NT, preferred_element_type=jnp.float32
                ) * (SHARPNESS * LOG2E)
                scores[pl.ds(k * LANES, 2 * LANES), pl.ds(start, 2 * LANES)] = product
                products_of[k // 2] = product
            lines = slice((k % 2) * LANES, (k % 2 + 1) * LANES)
            return products_of[k // 2][lines, half * LANES : (half + 1) * LANES]

        return block_of

    def shifted_blocks(start):
        def block_of(k, half):
            lines = pl.ds(k * LANES, LANES)
            return scores[lines, pl.ds(start + half * LANES, LANES)] + col_rep[lines, :]

        return block_of

    def first_plan(start, slot):
        block_of = first_blocks(start)
        for half in range(2):
            lanes = pl.ds(start + half * LANES, LANES)
            top = None
            for k in range(k_chunks):
                block = block_of(k, half) if half == 0 else scores[pl.ds(k * LANES, LANES), lanes]
                here = tree(jnp.maximum, [block[8 * n : 8 * n + 8] for n in range(LANES // 8)])
                top = here if top is None else jnp.maximum(top, here)
            top = jnp.max(top, axis=0, keepdims=True)
            total = None
            for k in range(k_chunks):
                value = jnp.exp2(scores[pl.ds(k * LANES, LANES), lanes] - top)
                scores[pl.ds(k * LANES, LANES), lanes] = value
                here = tree(jnp.add, [value[8 * n : 8 * n + 8] for n in range(LANES // 8)])
                total = here if total is None else total + here
            line = pl.ds(start // LANES + half, 1)
            row_share[line, :] = top
            slot[line, :] = top + log2(jnp.sum(total, axis=0, keepdims=True))

    def row_sums(start, slot):
        for half in range(2):
            lanes = pl.ds(start + half * LANES, LANES)
            sums = []
            for k in range(k_chunks):
                lines = pl.ds(k * LANES, LANES)
                value = scores[lines, lanes] * col_rep[lines, :]
                sums.append(tree(jnp.add, [value[8 * n : 8 * n + 8] for n in range(LANES // 8)]))
            line = pl.ds(start // LANES + half, 1)
            slot[line, :] = jnp.sum(tree(jnp.add, sums), axis=0, keepdims=True) * row_share[line, :]

    def poison(sums, least):
        inside = (sums >= least) & (sums <= 2.0**60)
        return jnp.sum(jnp.where(inside, 0.0, jnp.nan), keepdims=True)

    row_poison = jnp.zeros((1, 1), jnp.float32)
    col_poison = jnp.zeros((1, 1), jnp.float32)
    for iteration in range(ITERS):
        slots = row_slots.at[iteration]

        @pl.loop(0, i_chunks // 2)
        def _(chunk):
            start = pl.multiple_of(chunk * 2 * LANES, 2 * LANES)
            if not scaled:
                row_lse(start, slots.at[mine], shifted_blocks(start) if iteration else first_blocks(start))
            elif iteration == 0:
                first_plan(start, slots.at[mine])
            else:
                row_sums(start, slots.at[mine])

        if iteration == 0:
            pl.semaphore_wait(barrier, n_pts + n_cen - 2)
        exchange(slots, row_send.at[iteration], row_recv.at[iteration], "cen", n_cen)
        if not scaled:
            row_potential = -math.log2(total_points) - merged_lse(slots[...])
        elif iteration == 0:
            share = jnp.exp2(row_share[...] - merged_lse(slots[...]))
            row_share[...] = share
            row_potential = share * (1.0 / total_points)
        else:
            sums = jnp.sum(slots[...], axis=0)
            row_poison = row_poison + poison(sums, 2.0**-30)
            row_potential = row_share[...] / (sums * float(total_points))
        for chunk in range(i_chunks):
            row_rep[:, pl.ds(chunk * LANES, LANES)] = jnp.broadcast_to(
                row_potential[chunk : chunk + 1, :], (8, LANES)
            )

        @pl.loop(0, n_k // 16, unroll=2)
        def _(group):
            start = pl.multiple_of(group * 16, 16)
            if scaled:
                parts = [
                    scores[pl.ds(start, 16), pl.ds(chunk * LANES, LANES)].reshape(2, 8, LANES)
                    * row_rep[:, pl.ds(chunk * LANES, LANES)][None]
                    for chunk in range(i_chunks)
                ]
                part_sum[pl.ds(start, 16), :] = tree(jnp.add, parts).reshape(16, LANES)
                return
            parts = [
                scores[pl.ds(start, 16), pl.ds(chunk * LANES, LANES)].reshape(2, 8, LANES)
                + row_rep[:, pl.ds(chunk * LANES, LANES)][None]
                for chunk in range(i_chunks)
            ]
            top = tree(jnp.maximum, parts)
            total = tree(jnp.add, [jnp.exp2(part - top) for part in parts])
            part_max[pl.ds(start, 16), :] = top.reshape(16, LANES)
            part_sum[pl.ds(start, 16), :] = total.reshape(16, LANES)

        slots = col_slots.at[iteration]
        for chunk in range(k_chunks):
            if scaled:
                sums = jnp.sum(part_sum[pl.ds(chunk * LANES, LANES), :].T, axis=0, keepdims=True)
                slots[me, pl.ds(chunk, 1), :] = sums + row_poison if iteration == ITERS - 1 else sums
                continue
            tops = part_max[pl.ds(chunk * LANES, LANES), :].T
            sums = part_sum[pl.ds(chunk * LANES, LANES), :].T
            top = jnp.max(tops, axis=0, keepdims=True)
            summed = jnp.sum(sums * jnp.exp2(tops - top), axis=0, keepdims=True)
            slots[me, pl.ds(chunk, 1), :] = top + log2(summed)
        exchange(slots, col_send.at[iteration], col_recv.at[iteration], "pts", n_pts)
        if scaled:
            sums = jnp.sum(slots[...], axis=0)
            col_poison = col_poison + poison(sums, 2.0**-60)
            col_potential = 1.0 / (sums * float(total_centroids))
        else:
            col_potential = -math.log2(total_centroids) - merged_lse(slots[...])
        for chunk in range(k_chunks):
            col_rep[pl.ds(chunk * LANES, LANES), :] = jnp.broadcast_to(
                col_potential[chunk : chunk + 1, :], (LANES, LANES)
            ).T

    mass_acc[...] = jnp.zeros_like(mass_acc)
    num_acc[...] = jnp.zeros_like(num_acc)

    def x_copy(part, group):
        return remote(
            x_out.at[part, group], x_in.at[part, group], xs_sem.at[part, group], xr_sem.at[part, group],
            "pts", 2 * hi + other,
        )

    def z_copy_to(part, group):
        return remote(
            z_out.at[part, group], z_in.at[part, hi], zs_sem.at[part, group], zr_sem.at[part, hi],
            "pts", 2 * group + lo,
        )

    def z_copy_from(part, group):
        return remote(
            z_out.at[part, group], z_in.at[part, group], zs_sem.at[part, group], zr_sem.at[part, group],
            "pts", 2 * group + lo,
        )

    def gx_copy(part, group, side):
        block = gathered.at[part, 2 * group + side]
        return remote(block, block, gxs_sem.at[part, group], gxr_sem.at[part, group], "pts", 2 * hi + other)

    def gz_copy_to(part, group):
        block = gathered.at[part, me]
        return remote(block, block, gzs_sem.at[part, group], gzr_sem.at[part, hi], "pts", 2 * group + lo)

    def gz_copy_from(part, group):
        block = gathered.at[part, 2 * group + lo]
        return remote(block, block, gzs_sem.at[part, group], gzr_sem.at[part, group], "pts", 2 * group + lo)

    def later(step):
        return lax.rem(hi + step + 1, groups)

    def earlier(step):
        return lax.rem(hi + groups - step - 1, groups)

    own_half = pl.ds(pl.multiple_of(lo * rows, rows), rows)
    other_half = pl.ds(pl.multiple_of(other * rows, rows), rows)

    def columns_of(part):
        return slice(part * piece, (part + 1) * piece)

    def plan(group):
        base = pl.multiple_of(group * pair, pair)

        @pl.loop(0, pair // 16)
        def _(sub):
            start = pl.multiple_of(base + sub * 16, 16)
            for chunk in range(i_chunks):
                lanes = pl.ds(chunk * LANES, LANES)
                value = scores[pl.ds(start, 16), lanes].reshape(2, 8, LANES)
                by_row, by_col = row_rep[:, lanes][None], col_rep[pl.ds(start, 16), :].reshape(2, 8, LANES)
                value = value * by_row * by_col if scaled else jnp.exp2(value + by_row + by_col)
                mass_acc[:, lanes] += value[0] + value[1]
                value = value.reshape(16, LANES)
                scores[pl.ds(start, 16), lanes] = value
                weights[pl.ds(start, 16), lanes] = value.astype(jnp.bfloat16)

    def produce(part):
        @pl.loop(0, groups)
        def _(step):
            group = later(step)
            if part == 0:
                plan(group)
            base = pl.multiple_of(group * pair, pair)
            products[part, group] = lax.dot_general(
                weights[pl.ds(base, pair), :], points[:, columns_of(part)], NN, preferred_element_type=jnp.float32
            )
            x_out[part, group] = products[part, group, other_half, :].astype(jnp.bfloat16)
            x_copy(part, group).start()

    def reduce_pair(part):
        @pl.loop(0, groups - 1)
        def _(step):
            group = later(step)
            x_copy(part, group).wait_recv()
            z_out[part, group] = (
                products[part, group, own_half, :] + x_in[part, group].astype(jnp.float32)
            ).astype(jnp.bfloat16)
            z_copy_to(part, group).start()

    def finish(part):
        x_copy(part, hi).wait_recv()
        products[part, hi, own_half, :] = products[part, hi, own_half, :] + x_in[part, hi].astype(jnp.float32)

        @pl.loop(0, groups - 1)
        def _(step):
            group = earlier(step)
            z_copy_from(part, group).wait_recv()
            products[part, hi, own_half, :] = products[part, hi, own_half, :] + z_in[part, group].astype(jnp.float32)

        done = (products[part, hi, own_half, :] * float(total_centroids)).astype(jnp.bfloat16)
        new_block[:, columns_of(part)] = done
        gathered[part, me] = done
        gx_copy(part, hi, lo).start()

        @pl.loop(0, groups - 1)
        def _(step):
            gz_copy_to(part, later(step)).start()

    def hand_on(part):
        @pl.loop(0, groups - 1)
        def _(step):
            group = earlier(step)
            gz_copy_from(part, group).wait_recv()
            gx_copy(part, group, lo).start()

    def cross(part):
        @pl.loop(0, groups)
        def _(step):
            group = lax.rem(hi + groups - step, groups)
            gx_copy(part, group, other).wait_recv()
            base = pl.multiple_of(group * pair, pair)
            block = gathered[part, pl.ds(2 * group, 2)].reshape(pair, piece)
            wide = block.astype(jnp.float32)
            squares = jnp.sum(wide * wide, axis=1, keepdims=True)
            doubled = (wide * -2.0).astype(jnp.bfloat16)

            @pl.loop(0, n_i // 512)
            def _(chunk):
                lanes = pl.ds(pl.multiple_of(chunk * 512, 512), 512)
                product = lax.dot_general(
                    doubled, points[lanes, columns_of(part)], NT, preferred_element_type=jnp.float32
                )
                terms = scores[pl.ds(base, pair), lanes] * (squares + product)
                num_acc[:, lanes] += jnp.sum(terms.reshape(pair // 8, 8, 512), axis=0)

    produce(0)
    for part in range(1, parts):
        produce(part)
        reduce_pair(part - 1)
        if part >= 2:
            finish(part - 2)
    reduce_pair(parts - 1)
    if parts >= 2:
        finish(parts - 2)
        hand_on(0)
    finish(parts - 1)
    for part in range(parts):
        if part or parts == 1:
            hand_on(part)
        cross(part)

    final = final_slots.at[mine]
    for chunk in range(i_chunks):
        lanes = pl.ds(chunk * LANES, LANES)
        final[pl.ds(chunk, 1), :] = jnp.sum(num_acc[:, lanes], axis=0, keepdims=True)
        final[pl.ds(i_chunks + chunk, 1), :] = (
            jnp.sum(mass_acc[:, lanes], axis=0, keepdims=True) + col_poison
        )
    exchange(final_slots, final_send, final_recv, "cen", n_cen)
    sums = jnp.sum(final_slots[...], axis=0)
    distances[...] = sums[:i_chunks] / sums[i_chunks:] / float(width)

    for part in range(parts):

        @pl.loop(0, groups)
        def _(step):
            x_copy(part, step).wait_send()
            gx_copy(part, step, lo).wait_send()

        @pl.loop(0, groups - 1)
        def _(step):
            z_copy_to(part, later(step)).wait_send()
            gz_copy_to(part, later(step)).wait_send()


def step_kernel(scaled, n_pts, n_cen, points, centroids):
    n_i, width = points.shape
    n_k = centroids.shape[0]
    rows, groups = n_k // n_pts, n_pts // 2
    i_chunks, k_chunks = n_i // LANES, n_k // LANES
    parts = 3 if width % (3 * LANES) == 0 else 1
    piece = width // parts
    f32, bf16 = jnp.float32, jnp.bfloat16
    vmem, dma = pltpu.VMEM, pltpu.SemaphoreType.DMA
    whole = pl.BlockSpec(memory_space=pltpu.VMEM)
    new_block, distances = pl.pallas_call(
        functools.partial(kernel, scaled, n_pts, n_cen, n_i * n_pts, n_k * n_cen),
        out_shape=(
            jax.ShapeDtypeStruct((rows, width), bf16),
            jax.ShapeDtypeStruct((i_chunks, LANES), f32),
        ),
        in_specs=[whole, whole],
        out_specs=(whole, whole),
        scratch_shapes=[
            vmem((n_k, n_i), f32),
            vmem((n_k, n_i), bf16),
            vmem((parts, groups, 2 * rows, piece), f32),
            vmem((ITERS, n_cen, i_chunks, LANES), f32),
            vmem((ITERS, n_pts, k_chunks, LANES), f32),
            vmem((n_cen, 2 * i_chunks, LANES), f32),
            vmem((8, n_i), f32),
            vmem((n_k, LANES), f32),
            vmem((n_k, LANES), f32),
            vmem((n_k, LANES), f32),
            vmem((i_chunks, LANES), f32),
            vmem((8, n_i), f32),
            vmem((8, n_i), f32),
            vmem((parts, groups, rows, piece), bf16),
            vmem((parts, groups, rows, piece), bf16),
            vmem((parts, groups, rows, piece), bf16),
            vmem((parts, groups, rows, piece), bf16),
            vmem((parts, n_pts, rows, piece), bf16),
            dma((ITERS, n_cen)), dma((ITERS, n_cen)),
            dma((ITERS, n_pts)), dma((ITERS, n_pts)),
            dma((n_cen,)), dma((n_cen,)),
            *[dma((parts, groups)) for _ in range(8)],
        ],
        compiler_params=pltpu.CompilerParams(
            collective_id=0 if scaled else 1, has_side_effects=True, vmem_limit_bytes=52 * 2**20
        ),
        cost_estimate=pl.CostEstimate(
            flops=6 * n_i * n_k * width, bytes_accessed=2 * (n_i + n_k) * width, transcendentals=7 * n_i * n_k
        ),
    )(points, centroids)
    return new_block, distances.reshape(n_i)


def on_device(n_pts, n_cen, points, centroids):
    new_block, distances = step_kernel(True, n_pts, n_cen, points, centroids)
    return lax.cond(
        distances[0] == distances[0],
        lambda *_: (new_block, distances),
        functools.partial(step_kernel, False, n_pts, n_cen),
        points, centroids,
    )


def solution(mesh):
    n_pts, n_cen = mesh.shape["pts"], mesh.shape["cen"]
    return jax.shard_map(
        functools.partial(on_device, n_pts, n_cen),
        mesh=mesh,
        in_specs=(P("pts", None), P("cen", None)),
        out_specs=(P(("cen", "pts"), None), P("pts")),
        check_vma=False,
    )
```

```python
import functools
import math

import jax
import jax.numpy as jnp
from jax import lax
from jax.experimental import pallas as pl
from jax.experimental.pallas import tpu as pltpu
from jax.sharding import PartitionSpec as P

ITERS = 3
SHARPNESS = 4.0
LOG2E = 1.4426950408889634
LANES = 128
NT = (((1,), (1,)), ((), ()))
NN = (((1,), (0,)), ((), ()))


def log2(value):
    return jnp.log(value) * LOG2E


def merged_lse(parts):
    highest = jnp.max(parts, axis=0)
    return highest + log2(jnp.sum(jnp.exp2(parts - highest[None]), axis=0))


def remote(src, dst, send, recv, axis, index):
    return pltpu.make_async_remote_copy(
        src_ref=src, dst_ref=dst, send_sem=send, recv_sem=recv,
        device_id={axis: index}, device_id_type=pl.DeviceIdType.MESH,
    )


def each(start, stop, body):
    if stop - start <= 8:
        for step in range(start, stop):
            body(step)
    else:
        pl.loop(start, stop)(body)


def tree(join, values):
    values = list(values)
    while len(values) > 1:
        paired = [join(a, b) for a, b in zip(values[::2], values[1::2])]
        values = paired + values[len(values) & ~1 :]
    return values[0]


def exchange(slots, send, recv, axis, count):
    me = lax.axis_index(axis)

    def copy_to(step):
        peer = lax.rem(me + step, count)
        return remote(slots.at[me], slots.at[me], send.at[peer], recv.at[me], axis, peer)

    def copy_from(step):
        peer = lax.rem(me + step, count)
        return remote(slots.at[peer], slots.at[peer], send.at[peer], recv.at[peer], axis, peer)

    each(1, count, lambda step: copy_to(step).start())
    each(1, count, lambda step: copy_from(step).wait_recv())
    return lambda: each(1, count, lambda step: copy_to(step).wait_send())


def kernel(
    scaled, n_pts, n_cen, total_points, total_centroids,
    points, centroids, new_block, distances,
    scores, weights, products, row_slots, col_slots, final_slots, row_rep, col_rep, part_max, part_sum, row_share,
    mass_acc, num_acc, x_out, x_in, z_out, z_in, gathered,
    row_send, row_recv, col_send, col_recv, final_send, final_recv,
    xs_sem, xr_sem, zs_sem, zr_sem, gxs_sem, gxr_sem, gzs_sem, gzr_sem,
):
    n_i, width = points.shape
    n_k = centroids.shape[0]
    rows = n_k // n_pts
    pair = 2 * rows
    parts, piece = gathered.shape[0], gathered.shape[3]
    groups = n_pts // 2
    i_chunks = n_i // LANES
    k_chunks = n_k // LANES
    me = lax.axis_index("pts")
    mine = lax.axis_index("cen")
    hi = me // 2
    lo = lax.rem(me, 2)
    other = 1 - lo

    barrier = pltpu.get_barrier_semaphore()

    @pl.loop(1, n_pts)
    def _(step):
        pl.semaphore_signal(
            barrier, inc=1, device_id={"pts": lax.rem(me + step, n_pts)}, device_id_type=pl.DeviceIdType.MESH
        )

    @pl.loop(1, n_cen)
    def _(step):
        pl.semaphore_signal(
            barrier, inc=1, device_id={"cen": lax.rem(mine + step, n_cen)}, device_id_type=pl.DeviceIdType.MESH
        )

    def row_lse(start, slot, block_of):
        highest = [None, None]
        total = [None, None]
        for k in range(k_chunks):
            for half in range(2):
                block = block_of(k, half)
                parts = [block[8 * n : 8 * n + 8] for n in range(LANES // 8)]
                top = tree(jnp.maximum, parts)
                if highest[half] is not None:
                    top = jnp.maximum(highest[half], top)
                summed = tree(jnp.add, [jnp.exp2(part - top) for part in parts])
                if highest[half] is not None:
                    summed = total[half] * jnp.exp2(highest[half] - top) + summed
                highest[half], total[half] = top, summed
        for half in range(2):
            top = jnp.max(highest[half], axis=0, keepdims=True)
            summed = jnp.sum(total[half] * jnp.exp2(highest[half] - top), axis=0, keepdims=True)
            slot[pl.ds(start // LANES + half, 1), :] = top + log2(summed)

    def first_blocks(start):
        columns = points[pl.ds(start, 2 * LANES), :]
        products_of = {}

        def block_of(k, half):
            if k % 2 == 0 and half == 0:
                product = lax.dot_general(
                    centroids[pl.ds(k * LANES, 2 * LANES), :], columns, NT, preferred_element_type=jnp.float32
                ) * (SHARPNESS * LOG2E)
                scores[pl.ds(k * LANES, 2 * LANES), pl.ds(start, 2 * LANES)] = product
                products_of[k // 2] = product
            lines = slice((k % 2) * LANES, (k % 2 + 1) * LANES)
            return products_of[k // 2][lines, half * LANES : (half + 1) * LANES]

        return block_of

    def shifted_blocks(start):
        def block_of(k, half):
            lines = pl.ds(k * LANES, LANES)
            return scores[lines, pl.ds(start + half * LANES, LANES)] + col_rep[lines, :]

        return block_of

    def first_plan(start, slot):
        block_of = first_blocks(start)
        for half in range(2):
            lanes = pl.ds(start + half * LANES, LANES)
            top = None
            for k in range(k_chunks):
                block = block_of(k, half) if half == 0 else scores[pl.ds(k * LANES, LANES), lanes]
                here = tree(jnp.maximum, [block[8 * n : 8 * n + 8] for n in range(LANES // 8)])
                top = here if top is None else jnp.maximum(top, here)
            top = jnp.max(top, axis=0, keepdims=True)
            total = None
            for k in range(k_chunks):
                value = jnp.exp2(scores[pl.ds(k * LANES, LANES), lanes] - top)
                scores[pl.ds(k * LANES, LANES), lanes] = value
                here = tree(jnp.add, [value[8 * n : 8 * n + 8] for n in range(LANES // 8)])
                total = here if total is None else total + here
            line = pl.ds(start // LANES + half, 1)
            row_share[line, :] = top
            slot[line, :] = top + log2(jnp.sum(total, axis=0, keepdims=True))

    def row_sums(start, slot):
        for half in range(2):
            lanes = pl.ds(start + half * LANES, LANES)
            sums = []
            for k in range(k_chunks):
                lines = pl.ds(k * LANES, LANES)
                value = scores[lines, lanes] * col_rep[lines, :]
                sums.append(tree(jnp.add, [value[8 * n : 8 * n + 8] for n in range(LANES // 8)]))
            line = pl.ds(start // LANES + half, 1)
            slot[line, :] = jnp.sum(tree(jnp.add, sums), axis=0, keepdims=True) * row_share[line, :]

    def poison(sums, least):
        inside = (sums >= least) & (sums <= 2.0**60)
        return jnp.sum(jnp.where(inside, 0.0, jnp.nan), keepdims=True)

    unsent = []
    row_poison = jnp.zeros((1, 1), jnp.float32)
    col_poison = jnp.zeros((1, 1), jnp.float32)
    for iteration in range(ITERS):
        slots = row_slots.at[iteration]

        @pl.loop(0, i_chunks // 2)
        def _(chunk):
            start = pl.multiple_of(chunk * 2 * LANES, 2 * LANES)
            if not scaled:
                row_lse(start, slots.at[mine], shifted_blocks(start) if iteration else first_blocks(start))
            elif iteration == 0:
                first_plan(start, slots.at[mine])
            else:
                row_sums(start, slots.at[mine])

        if iteration == 0:
            pl.semaphore_wait(barrier, n_pts + n_cen - 2)
        unsent += [exchange(slots, row_send.at[iteration], row_recv.at[iteration], "cen", n_cen)]
        if not scaled:
            row_potential = -math.log2(total_points) - merged_lse(slots[...])
        elif iteration == 0:
            share = jnp.exp2(row_share[...] - merged_lse(slots[...]))
            row_share[...] = share
            row_potential = share * (1.0 / total_points)
        else:
            sums = jnp.sum(slots[...], axis=0)
            row_poison = row_poison + poison(sums, 2.0**-30)
            row_potential = row_share[...] / (sums * float(total_points))
        for chunk in range(i_chunks):
            row_rep[:, pl.ds(chunk * LANES, LANES)] = jnp.broadcast_to(
                row_potential[chunk : chunk + 1, :], (8, LANES)
            )

        @pl.loop(0, n_k // 16, unroll=2)
        def _(group):
            start = pl.multiple_of(group * 16, 16)
            if scaled:
                parts = [
                    scores[pl.ds(start, 16), pl.ds(chunk * LANES, LANES)].reshape(2, 8, LANES)
                    * row_rep[:, pl.ds(chunk * LANES, LANES)][None]
                    for chunk in range(i_chunks)
                ]
                part_sum[pl.ds(start, 16), :] = tree(jnp.add, parts).reshape(16, LANES)
                return
            parts = [
                scores[pl.ds(start, 16), pl.ds(chunk * LANES, LANES)].reshape(2, 8, LANES)
                + row_rep[:, pl.ds(chunk * LANES, LANES)][None]
                for chunk in range(i_chunks)
            ]
            top = tree(jnp.maximum, parts)
            total = tree(jnp.add, [jnp.exp2(part - top) for part in parts])
            part_max[pl.ds(start, 16), :] = top.reshape(16, LANES)
            part_sum[pl.ds(start, 16), :] = total.reshape(16, LANES)

        slots = col_slots.at[iteration]
        for chunk in range(k_chunks):
            if scaled:
                sums = jnp.sum(part_sum[pl.ds(chunk * LANES, LANES), :].T, axis=0, keepdims=True)
                slots[me, pl.ds(chunk, 1), :] = sums + row_poison if iteration == ITERS - 1 else sums
                continue
            tops = part_max[pl.ds(chunk * LANES, LANES), :].T
            sums = part_sum[pl.ds(chunk * LANES, LANES), :].T
            top = jnp.max(tops, axis=0, keepdims=True)
            summed = jnp.sum(sums * jnp.exp2(tops - top), axis=0, keepdims=True)
            slots[me, pl.ds(chunk, 1), :] = top + log2(summed)
        unsent += [exchange(slots, col_send.at[iteration], col_recv.at[iteration], "pts", n_pts)]
        if scaled:
            sums = jnp.sum(slots[...], axis=0)
            col_poison = col_poison + poison(sums, 2.0**-60)
            col_potential = 1.0 / (sums * float(total_centroids))
        else:
            col_potential = -math.log2(total_centroids) - merged_lse(slots[...])
        for chunk in range(k_chunks):
            col_rep[pl.ds(chunk * LANES, LANES), :] = jnp.broadcast_to(
                col_potential[chunk : chunk + 1, :], (LANES, LANES)
            ).T

    mass_acc[...] = jnp.zeros_like(mass_acc)
    num_acc[...] = jnp.zeros_like(num_acc)

    def x_copy(part, group):
        return remote(
            x_out.at[part, group], x_in.at[part, group], xs_sem.at[part, group], xr_sem.at[part, group],
            "pts", 2 * hi + other,
        )

    def z_copy_to(part, group):
        return remote(
            z_out.at[part, group], z_in.at[part, hi], zs_sem.at[part, group], zr_sem.at[part, hi],
            "pts", 2 * group + lo,
        )

    def z_copy_from(part, group):
        return remote(
            z_out.at[part, group], z_in.at[part, group], zs_sem.at[part, group], zr_sem.at[part, group],
            "pts", 2 * group + lo,
        )

    def gx_copy(part, group, side):
        block = gathered.at[part, 2 * group + side]
        return remote(block, block, gxs_sem.at[part, group], gxr_sem.at[part, group], "pts", 2 * hi + other)

    def line_copy(part, side, group, direction):
        column = lo if side == 0 else other
        block = gathered.at[part, 2 * group + column]
        return remote(
            block, block, gzs_sem.at[4 * part + 2 * side + direction, group], gzr_sem.at[2 * part + side, group],
            "pts", 2 * (hi + 2 * direction - 1) + lo,
        )

    def along_line(part, side, group):
        @pl.when((group <= hi) & (hi + 1 < groups))
        def _():
            line_copy(part, side, group, 1).start()

        @pl.when((group >= hi) & (hi >= 1))
        def _():
            line_copy(part, side, group, 0).start()

    def nearest(step):
        near = jnp.minimum(hi, groups - 1 - hi)
        beside = hi + ((step + 1) // 2) * (2 * lax.rem(step + 1, 2) - 1)
        rest = jnp.where(hi <= groups - 1 - hi, step, groups - 1 - step)
        return jnp.where(step <= 2 * near, beside, rest)

    def lo_first(part):
        return parts > 1 and part == parts - 1

    def later(step):
        return lax.rem(hi + step + 1, groups)

    def earlier(step):
        return lax.rem(hi + groups - step - 1, groups)

    own_half = pl.ds(pl.multiple_of(lo * rows, rows), rows)
    other_half = pl.ds(pl.multiple_of(other * rows, rows), rows)

    def columns_of(part):
        return slice(part * piece, (part + 1) * piece)

    def plan(group):
        base = pl.multiple_of(group * pair, pair)

        @pl.loop(0, pair // 16)
        def _(sub):
            start = pl.multiple_of(base + sub * 16, 16)
            for chunk in range(i_chunks):
                lanes = pl.ds(chunk * LANES, LANES)
                value = scores[pl.ds(start, 16), lanes].reshape(2, 8, LANES)
                by_row, by_col = row_rep[:, lanes][None], col_rep[pl.ds(start, 16), :].reshape(2, 8, LANES)
                value = value * by_row * by_col if scaled else jnp.exp2(value + by_row + by_col)
                mass_acc[:, lanes] += value[0] + value[1]
                value = value.reshape(16, LANES)
                scores[pl.ds(start, 16), lanes] = value
                weights[pl.ds(start, 16), lanes] = value.astype(jnp.bfloat16)

    def produce(part):
        @pl.loop(0, groups)
        def _(step):
            group = later(step)
            if part == 0:
                plan(group)
            base = pl.multiple_of(group * pair, pair)
            products[part, group] = lax.dot_general(
                weights[pl.ds(base, pair), :], points[:, columns_of(part)], NN, preferred_element_type=jnp.float32
            )
            x_out[part, group] = products[part, group, other_half, :].astype(jnp.bfloat16)
            x_copy(part, group).start()

    def reduce_pair(part):
        @pl.loop(0, groups - 1)
        def _(step):
            group = later(step)
            x_copy(part, group).wait_recv()
            z_out[part, group] = (
                products[part, group, own_half, :] + x_in[part, group].astype(jnp.float32)
            ).astype(jnp.bfloat16)
            z_copy_to(part, group).start()

    def finish(part):
        x_copy(part, hi).wait_recv()
        products[part, hi, own_half, :] = products[part, hi, own_half, :] + x_in[part, hi].astype(jnp.float32)

        @pl.loop(0, groups - 1)
        def _(step):
            group = earlier(step)
            z_copy_from(part, group).wait_recv()
            products[part, hi, own_half, :] = products[part, hi, own_half, :] + z_in[part, group].astype(jnp.float32)

        done = (products[part, hi, own_half, :] * float(total_centroids)).astype(jnp.bfloat16)
        new_block[:, columns_of(part)] = done
        gathered[part, me] = done
        gx_copy(part, hi, lo).start()
        along_line(part, 0, hi)
        if lo_first(part):
            gx_copy(part, hi, other).wait_recv()
            along_line(part, 1, hi)

    def hand_on(part, step):
        group = nearest(step)
        for side in range(2 if lo_first(part) else 1):
            line_copy(part, side, group, 0).wait_recv()
            along_line(part, side, group)
        if not lo_first(part):
            gx_copy(part, group, lo).start()

    def cross(part, step):
        group = nearest(step)
        if not lo_first(part):
            gx_copy(part, group, other).wait_recv()
        base = pl.multiple_of(group * pair, pair)
        block = gathered[part, pl.ds(2 * group, 2)].reshape(pair, piece)
        wide = block.astype(jnp.float32)
        squares = jnp.sum(wide * wide, axis=1, keepdims=True)
        doubled = (wide * -2.0).astype(jnp.bfloat16)

        @pl.loop(0, n_i // 512)
        def _(chunk):
            lanes = pl.ds(pl.multiple_of(chunk * 512, 512), 512)
            product = lax.dot_general(
                doubled, points[lanes, columns_of(part)], NT, preferred_element_type=jnp.float32
            )
            terms = scores[pl.ds(base, pair), lanes] * (squares + product)
            num_acc[:, lanes] += jnp.sum(terms.reshape(pair // 8, 8, 512), axis=0)

    produce(0)
    for part in range(1, parts):
        produce(part)
        reduce_pair(part - 1)
        if part >= 2:
            finish(part - 2)
    reduce_pair(parts - 1)
    if parts == 3 and groups == 4:
        hand_on(0, 1)
        finish(1)
        hand_on(0, 2)
        hand_on(1, 1)
        cross(0, 0)
        hand_on(0, 3)
        hand_on(1, 2)
        cross(0, 1)
        finish(2)
        hand_on(1, 3)
        cross(0, 2)
        hand_on(2, 1)
        cross(0, 3)
        hand_on(2, 2)
        cross(1, 0)
        hand_on(2, 3)
        for step in range(1, 4):
            cross(1, step)
        for step in range(4):
            cross(2, step)
    else:
        if parts >= 2:
            finish(parts - 2)
        finish(parts - 1)
        for part in range(parts):
            pl.loop(1, groups)(functools.partial(hand_on, part))
            pl.loop(0, groups)(functools.partial(cross, part))

    final = final_slots.at[mine]
    for chunk in range(i_chunks):
        lanes = pl.ds(chunk * LANES, LANES)
        final[pl.ds(chunk, 1), :] = jnp.sum(num_acc[:, lanes], axis=0, keepdims=True)
        final[pl.ds(i_chunks + chunk, 1), :] = (
            jnp.sum(mass_acc[:, lanes], axis=0, keepdims=True) + col_poison
        )
    unsent += [exchange(final_slots, final_send, final_recv, "cen", n_cen)]
    sums = jnp.sum(final_slots[...], axis=0)
    distances[...] = sums[:i_chunks] / sums[i_chunks:] / float(width)

    for wait in unsent:
        wait()
    for part in range(parts):

        @pl.loop(0, groups)
        def _(step):
            x_copy(part, step).wait_send()
            if not lo_first(part):
                gx_copy(part, step, lo).wait_send()
            for side in range(2 if lo_first(part) else 1):

                @pl.when((step <= hi) & (hi + 1 < groups))
                def _():
                    line_copy(part, side, step, 1).wait_send()

                @pl.when((step >= hi) & (hi >= 1))
                def _():
                    line_copy(part, side, step, 0).wait_send()

        if lo_first(part):
            gx_copy(part, hi, lo).wait_send()

        @pl.loop(0, groups - 1)
        def _(step):
            z_copy_to(part, later(step)).wait_send()


def step_kernel(scaled, n_pts, n_cen, points, centroids):
    n_i, width = points.shape
    n_k = centroids.shape[0]
    rows, groups = n_k // n_pts, n_pts // 2
    i_chunks, k_chunks = n_i // LANES, n_k // LANES
    parts = 3 if width % (3 * LANES) == 0 else 1
    piece = width // parts
    f32, bf16 = jnp.float32, jnp.bfloat16
    vmem, dma = pltpu.VMEM, pltpu.SemaphoreType.DMA
    whole = pl.BlockSpec(memory_space=pltpu.VMEM)
    new_block, distances = pl.pallas_call(
        functools.partial(kernel, scaled, n_pts, n_cen, n_i * n_pts, n_k * n_cen),
        out_shape=(
            jax.ShapeDtypeStruct((rows, width), bf16),
            jax.ShapeDtypeStruct((i_chunks, LANES), f32),
        ),
        in_specs=[whole, whole],
        out_specs=(whole, whole),
        scratch_shapes=[
            vmem((n_k, n_i), f32),
            vmem((n_k, n_i), bf16),
            vmem((parts, groups, 2 * rows, piece), f32),
            vmem((ITERS, n_cen, i_chunks, LANES), f32),
            vmem((ITERS, n_pts, k_chunks, LANES), f32),
            vmem((n_cen, 2 * i_chunks, LANES), f32),
            vmem((8, n_i), f32),
            vmem((n_k, LANES), f32),
            vmem((n_k, LANES), f32),
            vmem((n_k, LANES), f32),
            vmem((i_chunks, LANES), f32),
            vmem((8, n_i), f32),
            vmem((8, n_i), f32),
            vmem((parts, groups, rows, piece), bf16),
            vmem((parts, groups, rows, piece), bf16),
            vmem((parts, groups, rows, piece), bf16),
            vmem((parts, groups, rows, piece), bf16),
            vmem((parts, n_pts, rows, piece), bf16),
            dma((ITERS, n_cen)), dma((ITERS, n_cen)),
            dma((ITERS, n_pts)), dma((ITERS, n_pts)),
            dma((n_cen,)), dma((n_cen,)),
            *[dma((parts, groups)) for _ in range(6)],
            dma((4 * parts, groups)),
            dma((2 * parts, groups)),
        ],
        compiler_params=pltpu.CompilerParams(
            collective_id=0 if scaled else 1, has_side_effects=True, vmem_limit_bytes=52 * 2**20
        ),
        cost_estimate=pl.CostEstimate(
            flops=6 * n_i * n_k * width, bytes_accessed=2 * (n_i + n_k) * width, transcendentals=7 * n_i * n_k
        ),
    )(points, centroids)
    return new_block, distances.reshape(n_i)


def on_device(n_pts, n_cen, points, centroids):
    new_block, distances = step_kernel(True, n_pts, n_cen, points, centroids)
    return lax.cond(
        distances[0] == distances[0],
        lambda *_: (new_block, distances),
        functools.partial(step_kernel, False, n_pts, n_cen),
        points, centroids,
    )


def solution(mesh):
    n_pts, n_cen = mesh.shape["pts"], mesh.shape["cen"]
    return jax.shard_map(
        functools.partial(on_device, n_pts, n_cen),
        mesh=mesh,
        in_specs=(P("pts", None), P("cen", None)),
        out_specs=(P(("cen", "pts"), None), P("pts")),
        check_vma=False,
    )
```

```python
import functools
import math

import jax
import jax.numpy as jnp
from jax import lax
from jax.experimental import pallas as pl
from jax.experimental.pallas import tpu as pltpu
from jax.sharding import PartitionSpec as P

ITERS = 3
SHARPNESS = 4.0
LOG2E = 1.4426950408889634
LANES = 128
NT = (((1,), (1,)), ((), ()))
NN = (((1,), (0,)), ((), ()))


def log2(value):
    return jnp.log(value) * LOG2E


def merged_lse(parts):
    highest = jnp.max(parts, axis=0)
    return highest + log2(jnp.sum(jnp.exp2(parts - highest[None]), axis=0))


def remote(src, dst, send, recv, axis, index):
    return pltpu.make_async_remote_copy(
        src_ref=src, dst_ref=dst, send_sem=send, recv_sem=recv,
        device_id={axis: index}, device_id_type=pl.DeviceIdType.MESH,
    )


def each(start, stop, body):
    if stop - start <= 8:
        for step in range(start, stop):
            body(step)
    else:
        pl.loop(start, stop)(body)


def tree(join, values):
    values = list(values)
    while len(values) > 1:
        paired = [join(a, b) for a, b in zip(values[::2], values[1::2])]
        values = paired + values[len(values) & ~1 :]
    return values[0]


def exchange(slots, send, recv, axis, count):
    me = lax.axis_index(axis)

    def copy_to(step):
        peer = lax.rem(me + step, count)
        return remote(slots.at[me], slots.at[me], send.at[peer], recv.at[me], axis, peer)

    def copy_from(step):
        peer = lax.rem(me + step, count)
        return remote(slots.at[peer], slots.at[peer], send.at[peer], recv.at[peer], axis, peer)

    each(1, count, lambda step: copy_to(step).start())
    each(1, count, lambda step: copy_from(step).wait_recv())
    return lambda: each(1, count, lambda step: copy_to(step).wait_send())


def kernel(
    scaled, n_pts, n_cen, total_points, total_centroids,
    points, centroids, new_block, distances,
    scores, weights, products, row_slots, col_slots, final_slots, row_rep, col_rep, part_max, part_sum, row_share,
    mass_acc, num_acc, x_out, x_in, z_out, z_in, gathered,
    row_send, row_recv, col_send, col_recv, final_send, final_recv,
    xs_sem, xr_sem, zs_sem, zr_sem, gxs_sem, gxr_sem, gzs_sem, gzr_sem,
):
    n_i, width = points.shape
    n_k = centroids.shape[0]
    rows = n_k // n_pts
    pair = 2 * rows
    parts, piece = gathered.shape[0], gathered.shape[3]
    groups = n_pts // 2
    i_chunks = n_i // LANES
    k_chunks = n_k // LANES
    me = lax.axis_index("pts")
    mine = lax.axis_index("cen")
    hi = me // 2
    lo = lax.rem(me, 2)
    other = 1 - lo

    barrier = pltpu.get_barrier_semaphore()

    @pl.loop(1, n_pts)
    def _(step):
        pl.semaphore_signal(
            barrier, inc=1, device_id={"pts": lax.rem(me + step, n_pts)}, device_id_type=pl.DeviceIdType.MESH
        )

    @pl.loop(1, n_cen)
    def _(step):
        pl.semaphore_signal(
            barrier, inc=1, device_id={"cen": lax.rem(mine + step, n_cen)}, device_id_type=pl.DeviceIdType.MESH
        )

    def row_lse(start, slot, block_of):
        highest = [None, None]
        total = [None, None]
        for k in range(k_chunks):
            for half in range(2):
                block = block_of(k, half)
                parts = [block[8 * n : 8 * n + 8] for n in range(LANES // 8)]
                top = tree(jnp.maximum, parts)
                if highest[half] is not None:
                    top = jnp.maximum(highest[half], top)
                summed = tree(jnp.add, [jnp.exp2(part - top) for part in parts])
                if highest[half] is not None:
                    summed = total[half] * jnp.exp2(highest[half] - top) + summed
                highest[half], total[half] = top, summed
        for half in range(2):
            top = jnp.max(highest[half], axis=0, keepdims=True)
            summed = jnp.sum(total[half] * jnp.exp2(highest[half] - top), axis=0, keepdims=True)
            slot[pl.ds(start // LANES + half, 1), :] = top + log2(summed)

    def first_blocks(start):
        columns = points[pl.ds(start, 2 * LANES), :]
        products_of = {}

        def block_of(k, half):
            if k % 2 == 0 and half == 0:
                product = lax.dot_general(
                    centroids[pl.ds(k * LANES, 2 * LANES), :], columns, NT, preferred_element_type=jnp.float32
                ) * (SHARPNESS * LOG2E)
                scores[pl.ds(k * LANES, 2 * LANES), pl.ds(start, 2 * LANES)] = product
                products_of[k // 2] = product
            lines = slice((k % 2) * LANES, (k % 2 + 1) * LANES)
            return products_of[k // 2][lines, half * LANES : (half + 1) * LANES]

        return block_of

    def shifted_blocks(start):
        def block_of(k, half):
            lines = pl.ds(k * LANES, LANES)
            return scores[lines, pl.ds(start + half * LANES, LANES)] + col_rep[lines, :]

        return block_of

    def first_plan(start, slot):
        block_of = first_blocks(start)
        for half in range(2):
            lanes = pl.ds(start + half * LANES, LANES)
            top = None
            for k in range(k_chunks):
                block = block_of(k, half) if half == 0 else scores[pl.ds(k * LANES, LANES), lanes]
                here = tree(jnp.maximum, [block[8 * n : 8 * n + 8] for n in range(LANES // 8)])
                top = here if top is None else jnp.maximum(top, here)
            top = jnp.max(top, axis=0, keepdims=True)
            total = None
            for k in range(k_chunks):
                value = jnp.exp2(scores[pl.ds(k * LANES, LANES), lanes] - top)
                scores[pl.ds(k * LANES, LANES), lanes] = value
                here = tree(jnp.add, [value[8 * n : 8 * n + 8] for n in range(LANES // 8)])
                total = here if total is None else total + here
            line = pl.ds(start // LANES + half, 1)
            row_share[line, :] = top
            slot[line, :] = top + log2(jnp.sum(total, axis=0, keepdims=True))

    def row_sums(start, slot):
        for half in range(2):
            lanes = pl.ds(start + half * LANES, LANES)
            sums = []
            for k in range(k_chunks):
                lines = pl.ds(k * LANES, LANES)
                value = scores[lines, lanes] * col_rep[lines, :]
                sums.append(tree(jnp.add, [value[8 * n : 8 * n + 8] for n in range(LANES // 8)]))
            line = pl.ds(start // LANES + half, 1)
            slot[line, :] = jnp.sum(tree(jnp.add, sums), axis=0, keepdims=True) * row_share[line, :]

    def poison(sums, least):
        inside = (sums >= least) & (sums <= 2.0**60)
        return jnp.sum(jnp.where(inside, 0.0, jnp.nan), keepdims=True)

    unsent = []
    row_poison = jnp.zeros((1, 1), jnp.float32)
    col_poison = jnp.zeros((1, 1), jnp.float32)
    for iteration in range(ITERS):
        slots = row_slots.at[iteration]

        @pl.loop(0, i_chunks // 2)
        def _(chunk):
            start = pl.multiple_of(chunk * 2 * LANES, 2 * LANES)
            if not scaled:
                row_lse(start, slots.at[mine], shifted_blocks(start) if iteration else first_blocks(start))
            elif iteration == 0:
                first_plan(start, slots.at[mine])
            else:
                row_sums(start, slots.at[mine])

        if iteration == 0:
            pl.semaphore_wait(barrier, n_pts + n_cen - 2)
        unsent += [exchange(slots, row_send.at[iteration], row_recv.at[iteration], "cen", n_cen)]
        if not scaled:
            row_potential = -math.log2(total_points) - merged_lse(slots[...])
        elif iteration == 0:
            share = jnp.exp2(row_share[...] - merged_lse(slots[...]))
            row_share[...] = share
            row_potential = share * (1.0 / total_points)
        else:
            sums = jnp.sum(slots[...], axis=0)
            row_poison = row_poison + poison(sums, 2.0**-30)
            row_potential = row_share[...] / (sums * float(total_points))
        for chunk in range(i_chunks):
            row_rep[:, pl.ds(chunk * LANES, LANES)] = jnp.broadcast_to(
                row_potential[chunk : chunk + 1, :], (8, LANES)
            )

        @pl.loop(0, n_k // 16, unroll=2)
        def _(group):
            start = pl.multiple_of(group * 16, 16)
            if scaled:
                parts = [
                    scores[pl.ds(start, 16), pl.ds(chunk * LANES, LANES)].reshape(2, 8, LANES)
                    * row_rep[:, pl.ds(chunk * LANES, LANES)][None]
                    for chunk in range(i_chunks)
                ]
                part_sum[pl.ds(start, 16), :] = tree(jnp.add, parts).reshape(16, LANES)
                return
            parts = [
                scores[pl.ds(start, 16), pl.ds(chunk * LANES, LANES)].reshape(2, 8, LANES)
                + row_rep[:, pl.ds(chunk * LANES, LANES)][None]
                for chunk in range(i_chunks)
            ]
            top = tree(jnp.maximum, parts)
            total = tree(jnp.add, [jnp.exp2(part - top) for part in parts])
            part_max[pl.ds(start, 16), :] = top.reshape(16, LANES)
            part_sum[pl.ds(start, 16), :] = total.reshape(16, LANES)

        slots = col_slots.at[iteration]
        for chunk in range(k_chunks):
            if scaled:
                sums = jnp.sum(part_sum[pl.ds(chunk * LANES, LANES), :].T, axis=0, keepdims=True)
                slots[me, pl.ds(chunk, 1), :] = sums + row_poison if iteration == ITERS - 1 else sums
                continue
            tops = part_max[pl.ds(chunk * LANES, LANES), :].T
            sums = part_sum[pl.ds(chunk * LANES, LANES), :].T
            top = jnp.max(tops, axis=0, keepdims=True)
            summed = jnp.sum(sums * jnp.exp2(tops - top), axis=0, keepdims=True)
            slots[me, pl.ds(chunk, 1), :] = top + log2(summed)
        unsent += [exchange(slots, col_send.at[iteration], col_recv.at[iteration], "pts", n_pts)]
        if scaled:
            sums = jnp.sum(slots[...], axis=0)
            col_poison = col_poison + poison(sums, 2.0**-60)
            col_potential = 1.0 / (sums * float(total_centroids))
        else:
            col_potential = -math.log2(total_centroids) - merged_lse(slots[...])
        for chunk in range(k_chunks):
            col_rep[pl.ds(chunk * LANES, LANES), :] = jnp.broadcast_to(
                col_potential[chunk : chunk + 1, :], (LANES, LANES)
            ).T

    mass_acc[...] = jnp.zeros_like(mass_acc)
    num_acc[...] = jnp.zeros_like(num_acc)

    def x_copy(part, group):
        return remote(
            x_out.at[part, group], x_in.at[part, group], xs_sem.at[part, group], xr_sem.at[part, group],
            "pts", 2 * hi + other,
        )

    def z_copy_to(part, group):
        return remote(
            z_out.at[part, group], z_in.at[part, hi], zs_sem.at[part, group], zr_sem.at[part, hi],
            "pts", 2 * group + lo,
        )

    def z_copy_from(part, group):
        return remote(
            z_out.at[part, group], z_in.at[part, group], zs_sem.at[part, group], zr_sem.at[part, group],
            "pts", 2 * group + lo,
        )

    def gx_copy(part, group, side):
        block = gathered.at[part, 2 * group + side]
        return remote(block, block, gxs_sem.at[part, group], gxr_sem.at[part, group], "pts", 2 * hi + other)

    def gz_copy_to(part, group):
        block = gathered.at[part, me]
        return remote(block, block, gzs_sem.at[part, group], gzr_sem.at[part, hi], "pts", 2 * group + lo)

    def gz_copy_from(part, group):
        block = gathered.at[part, 2 * group + lo]
        return remote(block, block, gzs_sem.at[part, group], gzr_sem.at[part, group], "pts", 2 * group + lo)

    def later(step):
        return lax.rem(hi + step + 1, groups)

    def earlier(step):
        return lax.rem(hi + groups - step - 1, groups)

    own_half = pl.ds(pl.multiple_of(lo * rows, rows), rows)
    other_half = pl.ds(pl.multiple_of(other * rows, rows), rows)

    def columns_of(part):
        return slice(part * piece, (part + 1) * piece)

    def plan(group):
        base = pl.multiple_of(group * pair, pair)

        @pl.loop(0, pair // 16)
        def _(sub):
            start = pl.multiple_of(base + sub * 16, 16)
            for chunk in range(i_chunks):
                lanes = pl.ds(chunk * LANES, LANES)
                value = scores[pl.ds(start, 16), lanes].reshape(2, 8, LANES)
                by_row, by_col = row_rep[:, lanes][None], col_rep[pl.ds(start, 16), :].reshape(2, 8, LANES)
                value = value * by_row * by_col if scaled else jnp.exp2(value + by_row + by_col)
                mass_acc[:, lanes] += value[0] + value[1]
                value = value.reshape(16, LANES)
                scores[pl.ds(start, 16), lanes] = value
                weights[pl.ds(start, 16), lanes] = value.astype(jnp.bfloat16)

    def produce(part):
        @pl.loop(0, groups)
        def _(step):
            group = later(step)
            if part == 0:
                plan(group)
            base = pl.multiple_of(group * pair, pair)
            products[part, group] = lax.dot_general(
                weights[pl.ds(base, pair), :], points[:, columns_of(part)], NN, preferred_element_type=jnp.float32
            )
            x_out[part, group] = products[part, group, other_half, :].astype(jnp.bfloat16)
            x_copy(part, group).start()

    def reduce_pair(part):
        @pl.loop(0, groups - 1)
        def _(step):
            group = later(step)
            x_copy(part, group).wait_recv()
            z_out[part, group] = (
                products[part, group, own_half, :] + x_in[part, group].astype(jnp.float32)
            ).astype(jnp.bfloat16)
            z_copy_to(part, group).start()

    def finish(part):
        x_copy(part, hi).wait_recv()
        products[part, hi, own_half, :] = products[part, hi, own_half, :] + x_in[part, hi].astype(jnp.float32)

        @pl.loop(0, groups - 1)
        def _(step):
            group = earlier(step)
            z_copy_from(part, group).wait_recv()
            products[part, hi, own_half, :] = products[part, hi, own_half, :] + z_in[part, group].astype(jnp.float32)

        done = (products[part, hi, own_half, :] * float(total_centroids)).astype(jnp.bfloat16)
        new_block[:, columns_of(part)] = done
        gathered[part, me] = done
        gx_copy(part, hi, lo).start()

        @pl.loop(0, groups - 1)
        def _(step):
            gz_copy_to(part, later(step)).start()

    def hand_on(part):
        @pl.loop(0, groups - 1)
        def _(step):
            group = earlier(step)
            gz_copy_from(part, group).wait_recv()
            gx_copy(part, group, lo).start()

    def cross(group):
        base = pl.multiple_of(group * pair, pair)
        blocks = []
        squares = jnp.zeros((pair, 1), jnp.float32)
        for part in range(parts):
            gx_copy(part, group, other).wait_recv()
            wide = gathered[part, pl.ds(2 * group, 2)].reshape(pair, piece).astype(jnp.float32)
            squares = squares + jnp.sum(wide * wide, axis=1, keepdims=True)
            blocks.append((wide * -2.0).astype(jnp.bfloat16))
        doubled = jnp.concatenate(blocks, axis=1)

        @pl.loop(0, n_i // 512)
        def _(chunk):
            lanes = pl.ds(pl.multiple_of(chunk * 512, 512), 512)
            product = lax.dot_general(doubled, points[lanes, :], NT, preferred_element_type=jnp.float32)
            terms = scores[pl.ds(base, pair), lanes] * (squares + product)
            num_acc[:, lanes] += jnp.sum(terms.reshape(pair // 8, 8, 512), axis=0)

    produce(0)
    for part in range(1, parts):
        produce(part)
        reduce_pair(part - 1)
        if part >= 2:
            finish(part - 2)
    reduce_pair(parts - 1)
    if parts >= 2:
        finish(parts - 2)
        hand_on(0)
    finish(parts - 1)
    for part in range(1 if parts >= 2 else 0, parts):
        hand_on(part)

    @pl.loop(0, groups)
    def _(step):
        cross(lax.rem(hi + groups - step, groups))

    final = final_slots.at[mine]
    for chunk in range(i_chunks):
        lanes = pl.ds(chunk * LANES, LANES)
        final[pl.ds(chunk, 1), :] = jnp.sum(num_acc[:, lanes], axis=0, keepdims=True)
        final[pl.ds(i_chunks + chunk, 1), :] = (
            jnp.sum(mass_acc[:, lanes], axis=0, keepdims=True) + col_poison
        )
    unsent += [exchange(final_slots, final_send, final_recv, "cen", n_cen)]
    sums = jnp.sum(final_slots[...], axis=0)
    distances[...] = sums[:i_chunks] / sums[i_chunks:] / float(width)

    for wait in unsent:
        wait()
    for part in range(parts):

        @pl.loop(0, groups)
        def _(step):
            x_copy(part, step).wait_send()
            gx_copy(part, step, lo).wait_send()

        @pl.loop(0, groups - 1)
        def _(step):
            z_copy_to(part, later(step)).wait_send()
            gz_copy_to(part, later(step)).wait_send()


def step_kernel(scaled, n_pts, n_cen, points, centroids):
    n_i, width = points.shape
    n_k = centroids.shape[0]
    rows, groups = n_k // n_pts, n_pts // 2
    i_chunks, k_chunks = n_i // LANES, n_k // LANES
    parts = 3 if width % (3 * LANES) == 0 else 1
    piece = width // parts
    f32, bf16 = jnp.float32, jnp.bfloat16
    vmem, dma = pltpu.VMEM, pltpu.SemaphoreType.DMA
    whole = pl.BlockSpec(memory_space=pltpu.VMEM)
    new_block, distances = pl.pallas_call(
        functools.partial(kernel, scaled, n_pts, n_cen, n_i * n_pts, n_k * n_cen),
        out_shape=(
            jax.ShapeDtypeStruct((rows, width), bf16),
            jax.ShapeDtypeStruct((i_chunks, LANES), f32),
        ),
        in_specs=[whole, whole],
        out_specs=(whole, whole),
        scratch_shapes=[
            vmem((n_k, n_i), f32),
            vmem((n_k, n_i), bf16),
            vmem((parts, groups, 2 * rows, piece), f32),
            vmem((ITERS, n_cen, i_chunks, LANES), f32),
            vmem((ITERS, n_pts, k_chunks, LANES), f32),
            vmem((n_cen, 2 * i_chunks, LANES), f32),
            vmem((8, n_i), f32),
            vmem((n_k, LANES), f32),
            vmem((n_k, LANES), f32),
            vmem((n_k, LANES), f32),
            vmem((i_chunks, LANES), f32),
            vmem((8, n_i), f32),
            vmem((8, n_i), f32),
            vmem((parts, groups, rows, piece), bf16),
            vmem((parts, groups, rows, piece), bf16),
            vmem((parts, groups, rows, piece), bf16),
            vmem((parts, groups, rows, piece), bf16),
            vmem((parts, n_pts, rows, piece), bf16),
            dma((ITERS, n_cen)), dma((ITERS, n_cen)),
            dma((ITERS, n_pts)), dma((ITERS, n_pts)),
            dma((n_cen,)), dma((n_cen,)),
            *[dma((parts, groups)) for _ in range(8)],
        ],
        compiler_params=pltpu.CompilerParams(
            collective_id=0 if scaled else 1, has_side_effects=True, vmem_limit_bytes=52 * 2**20
        ),
        cost_estimate=pl.CostEstimate(
            flops=6 * n_i * n_k * width, bytes_accessed=2 * (n_i + n_k) * width, transcendentals=7 * n_i * n_k
        ),
    )(points, centroids)
    return new_block, distances.reshape(n_i)


def on_device(n_pts, n_cen, points, centroids):
    new_block, distances = step_kernel(True, n_pts, n_cen, points, centroids)
    return lax.cond(
        distances[0] == distances[0],
        lambda *_: (new_block, distances),
        functools.partial(step_kernel, False, n_pts, n_cen),
        points, centroids,
    )


def solution(mesh):
    n_pts, n_cen = mesh.shape["pts"], mesh.shape["cen"]
    return jax.shard_map(
        functools.partial(on_device, n_pts, n_cen),
        mesh=mesh,
        in_specs=(P("pts", None), P("cen", None)),
        out_specs=(P(("cen", "pts"), None), P("pts")),
        check_vma=False,
    )
```

```python
import functools
import math

import jax
import jax.numpy as jnp
from jax import lax
from jax.experimental import pallas as pl
from jax.experimental.pallas import tpu as pltpu
from jax.sharding import PartitionSpec as P

ITERS = 3
SHARPNESS = 4.0
LOG2E = 1.4426950408889634
LANES = 128
NT = (((1,), (1,)), ((), ()))
NN = (((1,), (0,)), ((), ()))


def log2(value):
    return jnp.log(value) * LOG2E


def merged_lse(parts):
    highest = jnp.max(parts, axis=0)
    return highest + log2(jnp.sum(jnp.exp2(parts - highest[None]), axis=0))


def remote(src, dst, send, recv, axis, index):
    return pltpu.make_async_remote_copy(
        src_ref=src, dst_ref=dst, send_sem=send, recv_sem=recv,
        device_id={axis: index}, device_id_type=pl.DeviceIdType.MESH,
    )


def each(start, stop, body):
    if stop - start <= 8:
        for step in range(start, stop):
            body(step)
    else:
        pl.loop(start, stop)(body)


def tree(join, values):
    values = list(values)
    while len(values) > 1:
        paired = [join(a, b) for a, b in zip(values[::2], values[1::2])]
        values = paired + values[len(values) & ~1 :]
    return values[0]


def exchange(slots, send, recv, axis, count):
    me = lax.axis_index(axis)

    def copy_to(step):
        peer = lax.rem(me + step, count)
        return remote(slots.at[me], slots.at[me], send.at[peer], recv.at[me], axis, peer)

    def copy_from(step):
        peer = lax.rem(me + step, count)
        return remote(slots.at[peer], slots.at[peer], send.at[peer], recv.at[peer], axis, peer)

    each(1, count, lambda step: copy_to(step).start())
    each(1, count, lambda step: copy_from(step).wait_recv())
    return lambda: each(1, count, lambda step: copy_to(step).wait_send())


def kernel(
    scaled, n_pts, n_cen, total_points, total_centroids,
    points, centroids, new_block, distances,
    scores, weights, products, row_slots, col_slots, final_slots, row_rep, col_rep, part_max, part_sum, row_share,
    mass_acc, num_acc, x_out, x_in, z_out, z_in, gathered,
    row_send, row_recv, col_send, col_recv, final_send, final_recv,
    xs_sem, xr_sem, zs_sem, zr_sem, gxs_sem, gxr_sem, gzs_sem, gzr_sem,
):
    n_i, width = points.shape
    n_k = centroids.shape[0]
    rows = n_k // n_pts
    pair = 2 * rows
    parts, piece = gathered.shape[0], gathered.shape[3]
    groups = n_pts // 2
    i_chunks = n_i // LANES
    k_chunks = n_k // LANES
    me = lax.axis_index("pts")
    mine = lax.axis_index("cen")
    hi = me // 2
    lo = lax.rem(me, 2)
    other = 1 - lo

    barrier = pltpu.get_barrier_semaphore()

    @pl.loop(1, n_pts)
    def _(step):
        pl.semaphore_signal(
            barrier, inc=1, device_id={"pts": lax.rem(me + step, n_pts)}, device_id_type=pl.DeviceIdType.MESH
        )

    @pl.loop(1, n_cen)
    def _(step):
        pl.semaphore_signal(
            barrier, inc=1, device_id={"cen": lax.rem(mine + step, n_cen)}, device_id_type=pl.DeviceIdType.MESH
        )

    def row_lse(start, slot, block_of):
        highest = [None, None]
        total = [None, None]
        for k in range(k_chunks):
            for half in range(2):
                block = block_of(k, half)
                parts = [block[8 * n : 8 * n + 8] for n in range(LANES // 8)]
                top = tree(jnp.maximum, parts)
                if highest[half] is not None:
                    top = jnp.maximum(highest[half], top)
                summed = tree(jnp.add, [jnp.exp2(part - top) for part in parts])
                if highest[half] is not None:
                    summed = total[half] * jnp.exp2(highest[half] - top) + summed
                highest[half], total[half] = top, summed
        for half in range(2):
            top = jnp.max(highest[half], axis=0, keepdims=True)
            summed = jnp.sum(total[half] * jnp.exp2(highest[half] - top), axis=0, keepdims=True)
            slot[pl.ds(start // LANES + half, 1), :] = top + log2(summed)

    def first_blocks(start):
        columns = points[pl.ds(start, 2 * LANES), :]
        products_of = {}

        def block_of(k, half):
            if k % 2 == 0 and half == 0:
                product = lax.dot_general(
                    centroids[pl.ds(k * LANES, 2 * LANES), :], columns, NT, preferred_element_type=jnp.float32
                ) * (SHARPNESS * LOG2E)
                scores[pl.ds(k * LANES, 2 * LANES), pl.ds(start, 2 * LANES)] = product
                products_of[k // 2] = product
            lines = slice((k % 2) * LANES, (k % 2 + 1) * LANES)
            return products_of[k // 2][lines, half * LANES : (half + 1) * LANES]

        return block_of

    def shifted_blocks(start):
        def block_of(k, half):
            lines = pl.ds(k * LANES, LANES)
            return scores[lines, pl.ds(start + half * LANES, LANES)] + col_rep[lines, :]

        return block_of

    def first_plan(start, slot):
        block_of = first_blocks(start)
        for half in range(2):
            lanes = pl.ds(start + half * LANES, LANES)
            top = None
            for k in range(k_chunks):
                block = block_of(k, half) if half == 0 else scores[pl.ds(k * LANES, LANES), lanes]
                here = tree(jnp.maximum, [block[8 * n : 8 * n + 8] for n in range(LANES // 8)])
                top = here if top is None else jnp.maximum(top, here)
            top = jnp.max(top, axis=0, keepdims=True)
            total = None
            for k in range(k_chunks):
                value = jnp.exp2(scores[pl.ds(k * LANES, LANES), lanes] - top)
                scores[pl.ds(k * LANES, LANES), lanes] = value
                here = tree(jnp.add, [value[8 * n : 8 * n + 8] for n in range(LANES // 8)])
                total = here if total is None else total + here
            line = pl.ds(start // LANES + half, 1)
            row_share[line, :] = top
            slot[line, :] = top + log2(jnp.sum(total, axis=0, keepdims=True))

    def row_sums(start, slot):
        for half in range(2):
            lanes = pl.ds(start + half * LANES, LANES)
            sums = []
            for k in range(k_chunks):
                lines = pl.ds(k * LANES, LANES)
                value = scores[lines, lanes] * col_rep[lines, :]
                sums.append(tree(jnp.add, [value[8 * n : 8 * n + 8] for n in range(LANES // 8)]))
            line = pl.ds(start // LANES + half, 1)
            slot[line, :] = jnp.sum(tree(jnp.add, sums), axis=0, keepdims=True) * row_share[line, :]

    def poison(sums, least):
        inside = (sums >= least) & (sums <= 2.0**60)
        return jnp.sum(jnp.where(inside, 0.0, jnp.nan), keepdims=True)

    unsent = []
    row_poison = jnp.zeros((1, 1), jnp.float32)
    col_poison = jnp.zeros((1, 1), jnp.float32)
    for iteration in range(ITERS):
        slots = row_slots.at[iteration]

        if scaled and iteration == 0:
            for chunk in range(i_chunks // 2):
                first_plan(chunk * 2 * LANES, slots.at[mine])
        else:

            @pl.loop(0, i_chunks // 2)
            def _(chunk):
                start = pl.multiple_of(chunk * 2 * LANES, 2 * LANES)
                if scaled:
                    row_sums(start, slots.at[mine])
                else:
                    row_lse(start, slots.at[mine], shifted_blocks(start) if iteration else first_blocks(start))

        if iteration == 0:
            pl.semaphore_wait(barrier, n_pts + n_cen - 2)
        unsent += [exchange(slots, row_send.at[iteration], row_recv.at[iteration], "cen", n_cen)]
        if not scaled:
            row_potential = -math.log2(total_points) - merged_lse(slots[...])
        elif iteration == 0:
            share = jnp.exp2(row_share[...] - merged_lse(slots[...]))
            row_share[...] = share
            row_potential = share * (1.0 / total_points)
        else:
            sums = jnp.sum(slots[...], axis=0)
            row_poison = row_poison + poison(sums, 2.0**-30)
            row_potential = row_share[...] / (sums * float(total_points))
        for chunk in range(i_chunks):
            row_rep[:, pl.ds(chunk * LANES, LANES)] = jnp.broadcast_to(
                row_potential[chunk : chunk + 1, :], (8, LANES)
            )

        @pl.loop(0, n_k // 16, unroll=2)
        def _(group):
            start = pl.multiple_of(group * 16, 16)
            if scaled:
                parts = [
                    scores[pl.ds(start, 16), pl.ds(chunk * LANES, LANES)].reshape(2, 8, LANES)
                    * row_rep[:, pl.ds(chunk * LANES, LANES)][None]
                    for chunk in range(i_chunks)
                ]
                part_sum[pl.ds(start, 16), :] = tree(jnp.add, parts).reshape(16, LANES)
                return
            parts = [
                scores[pl.ds(start, 16), pl.ds(chunk * LANES, LANES)].reshape(2, 8, LANES)
                + row_rep[:, pl.ds(chunk * LANES, LANES)][None]
                for chunk in range(i_chunks)
            ]
            top = tree(jnp.maximum, parts)
            total = tree(jnp.add, [jnp.exp2(part - top) for part in parts])
            part_max[pl.ds(start, 16), :] = top.reshape(16, LANES)
            part_sum[pl.ds(start, 16), :] = total.reshape(16, LANES)

        slots = col_slots.at[iteration]
        for chunk in range(k_chunks):
            if scaled:
                sums = jnp.sum(part_sum[pl.ds(chunk * LANES, LANES), :].T, axis=0, keepdims=True)
                slots[me, pl.ds(chunk, 1), :] = sums + row_poison if iteration == ITERS - 1 else sums
                continue
            tops = part_max[pl.ds(chunk * LANES, LANES), :].T
            sums = part_sum[pl.ds(chunk * LANES, LANES), :].T
            top = jnp.max(tops, axis=0, keepdims=True)
            summed = jnp.sum(sums * jnp.exp2(tops - top), axis=0, keepdims=True)
            slots[me, pl.ds(chunk, 1), :] = top + log2(summed)
        unsent += [exchange(slots, col_send.at[iteration], col_recv.at[iteration], "pts", n_pts)]
        if scaled:
            sums = jnp.sum(slots[...], axis=0)
            col_poison = col_poison + poison(sums, 2.0**-60)
            col_potential = 1.0 / (sums * float(total_centroids))
        else:
            col_potential = -math.log2(total_centroids) - merged_lse(slots[...])
        for chunk in range(k_chunks):
            col_rep[pl.ds(chunk * LANES, LANES), :] = jnp.broadcast_to(
                col_potential[chunk : chunk + 1, :], (LANES, LANES)
            ).T

    mass_acc[...] = jnp.zeros_like(mass_acc)
    num_acc[...] = jnp.zeros_like(num_acc)

    def x_copy(part, group):
        return remote(
            x_out.at[part, group], x_in.at[part, group], xs_sem.at[part, group], xr_sem.at[part, group],
            "pts", 2 * hi + other,
        )

    def z_copy_to(part, group):
        return remote(
            z_out.at[part, group], z_in.at[part, hi], zs_sem.at[part, group], zr_sem.at[part, hi],
            "pts", 2 * group + lo,
        )

    def z_copy_from(part, group):
        return remote(
            z_out.at[part, group], z_in.at[part, group], zs_sem.at[part, group], zr_sem.at[part, group],
            "pts", 2 * group + lo,
        )

    def gx_copy(part, group, side):
        block = gathered.at[part, 2 * group + side]
        return remote(block, block, gxs_sem.at[part, group], gxr_sem.at[part, group], "pts", 2 * hi + other)

    def gz_copy_to(part, group):
        block = gathered.at[part, me]
        return remote(block, block, gzs_sem.at[part, group], gzr_sem.at[part, hi], "pts", 2 * group + lo)

    def gz_copy_from(part, group):
        block = gathered.at[part, 2 * group + lo]
        return remote(block, block, gzs_sem.at[part, group], gzr_sem.at[part, group], "pts", 2 * group + lo)

    def later(step):
        return lax.rem(hi + step + 1, groups)

    def earlier(step):
        return lax.rem(hi + groups - step - 1, groups)

    own_half = pl.ds(pl.multiple_of(lo * rows, rows), rows)
    other_half = pl.ds(pl.multiple_of(other * rows, rows), rows)

    def columns_of(part):
        return slice(part * piece, (part + 1) * piece)

    def plan(group):
        base = pl.multiple_of(group * pair, pair)

        @pl.loop(0, pair // 16)
        def _(sub):
            start = pl.multiple_of(base + sub * 16, 16)
            for chunk in range(i_chunks):
                lanes = pl.ds(chunk * LANES, LANES)
                value = scores[pl.ds(start, 16), lanes].reshape(2, 8, LANES)
                by_row, by_col = row_rep[:, lanes][None], col_rep[pl.ds(start, 16), :].reshape(2, 8, LANES)
                value = value * by_row * by_col if scaled else jnp.exp2(value + by_row + by_col)
                mass_acc[:, lanes] += value[0] + value[1]
                value = value.reshape(16, LANES)
                scores[pl.ds(start, 16), lanes] = value
                weights[pl.ds(start, 16), lanes] = value.astype(jnp.bfloat16)

    def produce(part):
        @pl.loop(0, groups)
        def _(step):
            group = later(step)
            if part == 0:
                plan(group)
            base = pl.multiple_of(group * pair, pair)
            products[part, group] = lax.dot_general(
                weights[pl.ds(base, pair), :], points[:, columns_of(part)], NN, preferred_element_type=jnp.float32
            )
            x_out[part, group] = products[part, group, other_half, :].astype(jnp.bfloat16)
            x_copy(part, group).start()

    def reduce_pair(part):
        @pl.loop(0, groups - 1)
        def _(step):
            group = later(step)
            x_copy(part, group).wait_recv()
            z_out[part, group] = (
                products[part, group, own_half, :] + x_in[part, group].astype(jnp.float32)
            ).astype(jnp.bfloat16)
            z_copy_to(part, group).start()

    def finish(part):
        x_copy(part, hi).wait_recv()
        products[part, hi, own_half, :] = products[part, hi, own_half, :] + x_in[part, hi].astype(jnp.float32)

        @pl.loop(0, groups - 1)
        def _(step):
            group = earlier(step)
            z_copy_from(part, group).wait_recv()
            products[part, hi, own_half, :] = products[part, hi, own_half, :] + z_in[part, group].astype(jnp.float32)

        done = (products[part, hi, own_half, :] * float(total_centroids)).astype(jnp.bfloat16)
        new_block[:, columns_of(part)] = done
        gathered[part, me] = done
        gx_copy(part, hi, lo).start()

        @pl.loop(0, groups - 1)
        def _(step):
            gz_copy_to(part, later(step)).start()

    def hand_on(part):
        @pl.loop(0, groups - 1)
        def _(step):
            group = earlier(step)
            gz_copy_from(part, group).wait_recv()
            gx_copy(part, group, lo).start()

    def cross(group):
        base = pl.multiple_of(group * pair, pair)
        blocks = []
        squares = jnp.zeros((pair, 1), jnp.float32)
        for part in range(parts):
            gx_copy(part, group, other).wait_recv()
            wide = gathered[part, pl.ds(2 * group, 2)].reshape(pair, piece).astype(jnp.float32)
            squares = squares + jnp.sum(wide * wide, axis=1, keepdims=True)
            blocks.append((wide * -2.0).astype(jnp.bfloat16))
        doubled = jnp.concatenate(blocks, axis=1)

        @pl.loop(0, n_i // 512)
        def _(chunk):
            lanes = pl.ds(pl.multiple_of(chunk * 512, 512), 512)
            product = lax.dot_general(doubled, points[lanes, :], NT, preferred_element_type=jnp.float32)
            terms = scores[pl.ds(base, pair), lanes] * (squares + product)
            num_acc[:, lanes] += jnp.sum(terms.reshape(pair // 8, 8, 512), axis=0)

    produce(0)
    for part in range(1, parts):
        produce(part)
        reduce_pair(part - 1)
        if part >= 2:
            finish(part - 2)
    reduce_pair(parts - 1)
    if parts >= 2:
        finish(parts - 2)
        hand_on(0)
    finish(parts - 1)
    for part in range(1 if parts >= 2 else 0, parts):
        hand_on(part)

    @pl.loop(0, groups)
    def _(step):
        cross(lax.rem(hi + groups - step, groups))

    final = final_slots.at[mine]
    for chunk in range(i_chunks):
        lanes = pl.ds(chunk * LANES, LANES)
        final[pl.ds(chunk, 1), :] = jnp.sum(num_acc[:, lanes], axis=0, keepdims=True)
        final[pl.ds(i_chunks + chunk, 1), :] = (
            jnp.sum(mass_acc[:, lanes], axis=0, keepdims=True) + col_poison
        )
    unsent += [exchange(final_slots, final_send, final_recv, "cen", n_cen)]
    sums = jnp.sum(final_slots[...], axis=0)
    distances[...] = sums[:i_chunks] / sums[i_chunks:] / float(width)

    for wait in unsent:
        wait()
    for part in range(parts):

        @pl.loop(0, groups)
        def _(step):
            x_copy(part, step).wait_send()
            gx_copy(part, step, lo).wait_send()

        @pl.loop(0, groups - 1)
        def _(step):
            z_copy_to(part, later(step)).wait_send()
            gz_copy_to(part, later(step)).wait_send()


def step_kernel(scaled, n_pts, n_cen, points, centroids):
    n_i, width = points.shape
    n_k = centroids.shape[0]
    rows, groups = n_k // n_pts, n_pts // 2
    i_chunks, k_chunks = n_i // LANES, n_k // LANES
    parts = 3 if width % (3 * LANES) == 0 else 1
    piece = width // parts
    f32, bf16 = jnp.float32, jnp.bfloat16
    vmem, dma = pltpu.VMEM, pltpu.SemaphoreType.DMA
    whole = pl.BlockSpec(memory_space=pltpu.VMEM)
    new_block, distances = pl.pallas_call(
        functools.partial(kernel, scaled, n_pts, n_cen, n_i * n_pts, n_k * n_cen),
        out_shape=(
            jax.ShapeDtypeStruct((rows, width), bf16),
            jax.ShapeDtypeStruct((i_chunks, LANES), f32),
        ),
        in_specs=[whole, whole],
        out_specs=(whole, whole),
        scratch_shapes=[
            vmem((n_k, n_i), f32),
            vmem((n_k, n_i), bf16),
            vmem((parts, groups, 2 * rows, piece), f32),
            vmem((ITERS, n_cen, i_chunks, LANES), f32),
            vmem((ITERS, n_pts, k_chunks, LANES), f32),
            vmem((n_cen, 2 * i_chunks, LANES), f32),
            vmem((8, n_i), f32),
            vmem((n_k, LANES), f32),
            vmem((n_k, LANES), f32),
            vmem((n_k, LANES), f32),
            vmem((i_chunks, LANES), f32),
            vmem((8, n_i), f32),
            vmem((8, n_i), f32),
            vmem((parts, groups, rows, piece), bf16),
            vmem((parts, groups, rows, piece), bf16),
            vmem((parts, groups, rows, piece), bf16),
            vmem((parts, groups, rows, piece), bf16),
            vmem((parts, n_pts, rows, piece), bf16),
            dma((ITERS, n_cen)), dma((ITERS, n_cen)),
            dma((ITERS, n_pts)), dma((ITERS, n_pts)),
            dma((n_cen,)), dma((n_cen,)),
            *[dma((parts, groups)) for _ in range(8)],
        ],
        compiler_params=pltpu.CompilerParams(
            collective_id=0 if scaled else 1, has_side_effects=True, vmem_limit_bytes=52 * 2**20
        ),
        cost_estimate=pl.CostEstimate(
            flops=6 * n_i * n_k * width, bytes_accessed=2 * (n_i + n_k) * width, transcendentals=7 * n_i * n_k
        ),
    )(points, centroids)
    return new_block, distances.reshape(n_i)


def on_device(n_pts, n_cen, points, centroids):
    new_block, distances = step_kernel(True, n_pts, n_cen, points, centroids)
    return lax.cond(
        distances[0] == distances[0],
        lambda *_: (new_block, distances),
        functools.partial(step_kernel, False, n_pts, n_cen),
        points, centroids,
    )


def solution(mesh):
    n_pts, n_cen = mesh.shape["pts"], mesh.shape["cen"]
    return jax.shard_map(
        functools.partial(on_device, n_pts, n_cen),
        mesh=mesh,
        in_specs=(P("pts", None), P("cen", None)),
        out_specs=(P(("cen", "pts"), None), P("pts")),
        check_vma=False,
    )
```
